128 devices in a mesh: leaf: 32 (over x, y, core), sub: 4 (over z).
Axes of the slice: x: 4, y: 4, z: 4, core: 2. Of those that a mesh axis runs over, the one named last changes fastest.
Arguments:
- density: float32 [8192, 16, 128], P(('leaf', 'sub')), may hold values from -6 to 6
- leaf_basis: bfloat16 [8192, 32, 128], P(('leaf', 'sub')), may hold values from -0.5 to 0.5
- near_tiles: bfloat16 [16384, 128, 128], P(('leaf', 'sub')), may hold values from -0.5 to 0.5
- near_rows: int32 [16384], P(('leaf', 'sub')), may hold values from 0 to 8191, as said below
- near_cols: int32 [16384], P(('leaf', 'sub')), may hold values from 0 to 8191, as said below
- near_count: int32 [128], P(('leaf', 'sub')), may hold values from 16 to 128, as said below
- far_src: int32 [10880, 27], P(('leaf', 'sub')), may hold values from 0 to 8191, as said below
- coupling: bfloat16 [27, 10880, 1024], P(None, ('leaf', 'sub')), may hold values from -0.21875 to 0.21875
- transfer: float32 [10880, 1024], P(('leaf', 'sub')), may hold values from -0.75 to 0.75
- far_src_top: int32 [42, 27], replicated, may hold values from 0 to 31, as said below
- coupling_top: bfloat16 [42, 27, 1024], replicated, may hold values from -0.21875 to 0.21875
- transfer_top: float32 [42, 1024], replicated, may hold values from -0.75 to 0.75
Outputs:
- potential: float32 [8192, 16, 128], P(('leaf', 'sub'))
The draws below stay inside these ranges and needn't reach their ends.
Inputs may be any that keep to these rules, and one draw needn't show every extreme that they name: `near_rows`: slots of device p name leaves of device p; on every device slot 0 names its first leaf and slot 1 its last leaf. `near_cols`: each entry lies within 32 leaves of the target leaf of its slot; slot 0 names the leaf before its target and slot 1 the leaf after it, where those exist (else the target itself). `near_count`: some device has all 128 slots live. `far_src`: sources of a level-k cluster are level-k clusters at most 64 / 4^k positions away from it; on each device and level, entry 0 of its first cluster is the cluster before it and entry 1 of its last cluster the cluster after it, where those exist (else the cluster itself). `far_src_top`: sources are clusters of the same upper level; on the lowest upper level cluster 0's entry 0 is the level's last cluster and its entry 1 is cluster 0.
All inputs are finite; a program needn't handle non-finite values.
Results may differ from the reference program's by a relative error of at most 0.0003.
Values sent between devices are 32-bit elements; how exact they have to be, the bound alone decides.
No kernel may reach another device: no remote copies, remote signals or barrier semaphores. Data moves between devices by JAX's collectives and lax.ppermute only.
A program may use at most 192 MiB of HBM per device.

```python
import jax
import jax.numpy as jnp
from jax import lax

LEAF = 128
RANK = 32
NRHS = 16
FAR = 27
LPD = 64
LEAVES = 8192
TILES = 128
LOC = 85
UPPER = 32
TOPC = 42
N_LEAF = 32
N_SUB = 4


def near_pairs(key):
    device_count = N_LEAF * N_SUB
    rim_width = LPD // 2
    slot_total = device_count * TILES
    position = jnp.arange(slot_total, dtype=jnp.int32)
    owner_id = position // TILES
    within = position % TILES
    local_pick = jax.random.randint(jax.random.fold_in(key, 1), (slot_total,), 0, LPD)
    local_pick = jnp.where(within == 0, 0, jnp.where(within == 1, LPD - 1, local_pick))
    row_ids = owner_id * LPD + local_pick
    offset = jax.random.randint(jax.random.fold_in(key, 2), (slot_total,), -rim_width, rim_width + 1)
    offset = jnp.where(within == 0, -1, jnp.where(within == 1, 1, offset))
    col_ids = jnp.clip(row_ids + offset, 0, LEAVES - 1)
    return (row_ids.astype(jnp.int32), col_ids.astype(jnp.int32))


def draw_near_rows(key, part):
    shared = near_pairs(key)
    return shared[0]


def draw_near_cols(key, part):
    shared = near_pairs(key)
    return shared[1]


def draw_near_count(key, part):
    key = jax.random.fold_in(key, 7)
    device_count = N_LEAF * N_SUB
    floor_count = max(2, TILES // 8)
    span_size = TILES - floor_count
    spread = jax.random.randint(jax.random.fold_in(key, 1), (device_count,), 0, span_size + 1)
    counts = floor_count + spread * spread // span_size
    fullest = jax.random.randint(jax.random.fold_in(key, 2), (), 0, device_count)
    counts = jnp.where(jnp.arange(device_count, dtype=jnp.int32) == fullest, TILES, counts)
    return counts.astype(jnp.int32)


def draw_far_src(key, part):
    key = jax.random.fold_in(key, 11)
    device_count = N_LEAF * N_SUB
    level_sizes = [LPD]
    while level_sizes[-1] % 4 == 0:
        level_sizes.append(level_sizes[-1] // 4)
    blocks = []
    for level_idx in range(len(level_sizes)):
        level_size = level_sizes[level_idx]
        total_here = device_count * level_size
        target = jnp.arange(total_here, dtype=jnp.int32)
        offset = jax.random.randint(jax.random.fold_in(key, level_idx), (total_here, FAR), -level_size, level_size + 1)
        chosen = target[:, None] + offset
        within = target % level_size
        first_col = jnp.where(within == 0, target - 1, chosen[:, 0])
        second_col = jnp.where(within == level_size - 1, target + 1, chosen[:, 1])
        chosen = jnp.concatenate([first_col[:, None], second_col[:, None], chosen[:, 2:]], axis=1)
        chosen = jnp.clip(chosen, 0, total_here - 1)
        blocks.append(chosen.reshape(device_count, level_size, FAR))
    return jnp.concatenate(blocks, axis=1).reshape(device_count * LOC, FAR).astype(jnp.int32)


def draw_far_src_top(key, part):
    key = jax.random.fold_in(key, 23)
    level_sizes = [UPPER]
    while level_sizes[-1] >= 4:
        level_sizes.append(level_sizes[-1] // 4)
    blocks = []
    for level_idx in range(len(level_sizes)):
        level_size = level_sizes[level_idx]
        chosen = jax.random.randint(jax.random.fold_in(key, level_idx), (level_size, FAR), 0, level_size)
        if level_idx == 0:
            chosen = chosen.at[0, 0].set(level_size - 1)
            chosen = chosen.at[0, 1].set(0)
        blocks.append(chosen)
    return jnp.concatenate(blocks, axis=0).astype(jnp.int32)


def block_levels(stream_key, shape, pieces, low, largest):
    loudness, own = 1.0, jax.random.fold_in(stream_key, 6)
    for axis_at, shards_of in pieces:
        heights = jnp.exp(jax.random.uniform(jax.random.fold_in(own, axis_at), (shards_of,), jnp.float32, low / len(pieces), largest / len(pieces)))
        loudness = loudness * jnp.repeat(heights, shape[axis_at] // shards_of).reshape([-1 if axis == axis_at else 1 for axis in range(len(shape))])
    return loudness


def bell_draw(own_key, extent, scale, bound, split=(), kind=jnp.bfloat16):
    level = block_levels(own_key, extent, split, -0.22, 0.18) if split else 1.0
    values = jax.random.normal(own_key, extent, jnp.float32) * scale * level
    return jnp.minimum(jnp.maximum(values, -bound), bound).astype(kind)


def setup_inputs(seed: int = 0) -> dict:
    streams_of = jax.random.split(jax.random.key(seed), 13)
    return {
        "density": bell_draw(streams_of[0], (LEAVES, NRHS, LEAF), 1.0, 6.0, ((0, 128),), jnp.float32),
        "leaf_basis": bell_draw(streams_of[1], (LEAVES, RANK, LEAF), LEAF ** -0.5, 0.5, ((0, 128),)),
        "near_tiles": bell_draw(streams_of[2], (N_LEAF * N_SUB * TILES, LEAF, LEAF), LEAF ** -0.5, 0.5, ((0, 128),)),
        "near_rows": draw_near_rows(jax.random.fold_in(streams_of[12], 71), 0),
        "near_cols": draw_near_cols(jax.random.fold_in(streams_of[12], 71), 0),
        "near_count": draw_near_count(jax.random.fold_in(streams_of[12], 71), 0),
        "far_src": draw_far_src(jax.random.fold_in(streams_of[12], 71), 0),
        "coupling": bell_draw(streams_of[7], (FAR, N_LEAF * N_SUB * LOC, RANK * RANK), (FAR * RANK) ** -0.5, 0.21875, ((1, 128),)),
        "transfer": bell_draw(streams_of[8], (N_LEAF * N_SUB * LOC, RANK * RANK), (2 * RANK) ** -0.5, 0.75, ((0, 128),), jnp.float32),
        "far_src_top": draw_far_src_top(jax.random.fold_in(streams_of[12], 71), 0),
        "coupling_top": bell_draw(streams_of[10], (TOPC, FAR, RANK * RANK), (FAR * RANK) ** -0.5, 0.21875),
        "transfer_top": bell_draw(streams_of[11], (TOPC, RANK * RANK), (2 * RANK) ** -0.5, 0.75, (), jnp.float32),
    }


def level_plan(leaf_count, device_count):
    local_sizes = [leaf_count]
    while local_sizes[-1] % 4 == 0:
        local_sizes.append(local_sizes[-1] // 4)
    top_sizes = [device_count * local_sizes[-1] // 4]
    while top_sizes[-1] >= 4:
        top_sizes.append(top_sizes[-1] // 4)
    return local_sizes, top_sizes


def parent_sum(moments, transfers):
    contrib = jnp.einsum("nsr,nrq->nsq", moments, transfers, precision=lax.Precision.HIGHEST)
    return contrib.reshape((-1, 4) + contrib.shape[1:]).sum(axis=1)


def child_push(parents, transfers):
    repeated = jnp.repeat(parents, 4, axis=0)
    return jnp.einsum("nsq,nrq->nsr", repeated, transfers, precision=lax.Precision.HIGHEST)


def couple_terms(moments, sources, matrices):
    rank_size = moments.shape[2]
    gathered = jnp.take(moments, sources, axis=0)
    shaped = matrices.astype(jnp.float32).reshape(matrices.shape[:2] + (rank_size, rank_size))
    return jnp.einsum("nfrq,nfsq->nsr", shaped, gathered, precision=lax.Precision.HIGHEST)


def couple_lists(moments, sources, matrices):
    rank_size = moments.shape[2]
    total = jnp.zeros((sources.shape[0], moments.shape[1], rank_size), jnp.float32)
    for entry in range(sources.shape[1]):
        gathered = jnp.take(moments, sources[:, entry], axis=0)
        shaped = matrices[entry].astype(jnp.float32).reshape(-1, rank_size, rank_size)
        total = total + jnp.einsum("nsq,nrq->nsr", gathered, shaped, precision=lax.Precision.HIGHEST)
    return total


def crown_solve(first_moments, top_sizes, sources, matrices, transfers):
    rank_size = first_moments.shape[2]
    offsets = [sum(top_sizes[:level_idx]) for level_idx in range(len(top_sizes))]

    def trans_of(level_idx):
        begin_at = offsets[level_idx]
        return transfers[begin_at:begin_at + top_sizes[level_idx]].reshape(-1, rank_size, rank_size)

    moment_list = [first_moments]
    for level_idx in range(len(top_sizes) - 1):
        moment_list.append(parent_sum(moment_list[level_idx], trans_of(level_idx)))
    fields = []
    for level_idx in range(len(top_sizes)):
        begin_at = offsets[level_idx]
        end_at = begin_at + top_sizes[level_idx]
        fields.append(couple_terms(moment_list[level_idx], sources[begin_at:end_at], matrices[begin_at:end_at]))
    coeffs = fields[-1]
    for level_idx in reversed(range(len(top_sizes) - 1)):
        coeffs = fields[level_idx] + child_push(coeffs, trans_of(level_idx))
    return coeffs


def reference(density, leaf_basis, near_tiles, near_rows, near_cols, near_count, far_src, coupling, transfer, far_src_top, coupling_top, transfer_top):
    highest = lax.Precision.HIGHEST
    device_count = N_LEAF * N_SUB
    local_sizes, top_sizes = level_plan(LPD, device_count)
    rank_size = leaf_basis.shape[1]
    local_total = sum(local_sizes)
    starts = [sum(local_sizes[:level_idx]) for level_idx in range(len(local_sizes))]

    def per_level(array, level_idx):
        shaped = array.reshape((device_count, local_total) + array.shape[1:])
        picked = shaped[:, starts[level_idx]:starts[level_idx] + local_sizes[level_idx]]
        return picked.reshape((device_count * local_sizes[level_idx],) + array.shape[1:])

    def level_trans(level_idx):
        return per_level(transfer, level_idx).reshape(-1, rank_size, rank_size)

    basis_wide = leaf_basis.astype(jnp.float32)
    moment_list = [jnp.einsum("csj,crj->csr", density, basis_wide, precision=highest)]
    for level_idx in range(len(local_sizes) - 1):
        moment_list.append(parent_sum(moment_list[level_idx], level_trans(level_idx)))
    last_level = len(local_sizes) - 1
    crown_first = parent_sum(moment_list[last_level], level_trans(last_level))
    coeffs = crown_solve(crown_first, top_sizes, far_src_top, coupling_top, transfer_top)
    coupling_blocks = coupling.reshape(FAR, device_count, local_total, rank_size * rank_size)
    for level_idx in reversed(range(len(local_sizes))):
        level_size = local_sizes[level_idx]
        source_blocks = per_level(far_src, level_idx).reshape(device_count, level_size, FAR)
        matrix_blocks = coupling_blocks[:, :, starts[level_idx]:starts[level_idx] + level_size]
        matrix_blocks = jnp.transpose(matrix_blocks, (1, 0, 2, 3))
        current = moment_list[level_idx]
        level_field = lax.map(lambda packed: couple_lists(current, packed[0], packed[1]), (source_blocks, matrix_blocks))
        level_field = level_field.reshape((device_count * level_size,) + level_field.shape[2:])
        coeffs = level_field + child_push(coeffs, level_trans(level_idx))
    far_part = jnp.einsum("csr,cri->csi", coeffs, basis_wide, precision=highest)

    tile_blocks = near_tiles.reshape(device_count, TILES, LEAF, LEAF)
    row_blocks = near_rows.reshape(device_count, TILES)
    col_blocks = near_cols.reshape(device_count, TILES)
    owner_ids = jnp.arange(device_count).astype(jnp.int32)
    slot_ids = jnp.arange(TILES).astype(jnp.int32)

    def near_device(packed):
        tile_set, row_set, col_set, live_count, owner_id = packed
        sources = jnp.take(density, col_set, axis=0)
        products = jnp.einsum("tsj,tij->tsi", sources, tile_set.astype(jnp.float32), precision=highest)
        alive_mask = (slot_ids < live_count).astype(jnp.float32)
        products = products * alive_mask[:, None, None]
        return jax.ops.segment_sum(products, row_set - owner_id * LPD, num_segments=LPD)

    near_part = lax.map(near_device, (tile_blocks, row_blocks, col_blocks, near_count, owner_ids))
    near_part = near_part.reshape(density.shape)
    return near_part + far_part
```

```python
import jax
import jax.numpy as jnp
from jax import lax
from jax.experimental import pallas as pl
from jax.experimental.pallas import tpu as pltpu
from jax.sharding import PartitionSpec as P

f32, bf16 = jnp.float32, jnp.bfloat16
AXES = ("leaf", "sub")
LEAVES = 64
HALO = 32
NRHS = 16
RANK = 32
FAR = 27
SLOTS = 128
LEVELS = (64, 16, 4, 1)
STARTS = (0, 64, 80, 84)
UPPER = (32, 8, 2)
UPPER_STARTS = (0, 32, 40)
TILES = 22
SPAN = 4 * TILES
PARAMS = pltpu.CompilerParams(vmem_limit_bytes=48 * 1024 * 1024)


def dot_nn(a, b):
    return lax.dot_general(a, b, (((1,), (0,)), ((), ())), preferred_element_type=f32)


def dot_nt(a, b):
    return lax.dot_general(a, b, (((1,), (1,)), ((), ())), preferred_element_type=f32)


def halves(x):
    high = x.astype(bf16)
    return high, (x - high.astype(f32)).astype(bf16)


def stacked(x):
    high, low = halves(x)
    return jnp.concatenate([high, low], axis=0)


def folded(x):
    half = x.shape[0] // 2
    return x[:half] + x[half:]


def grid_of(shape):
    return (
        lax.broadcasted_iota(jnp.int32, shape, 0),
        lax.broadcasted_iota(jnp.int32, shape, 1),
    )


def ones_where(mask):
    return jnp.where(mask, 1.0, 0.0).astype(bf16)


def natural_of(lane):
    return (lane // 32) * 32 + 4 * (lane % 8) + (lane % 32) // 8


def mixing():
    x, y = grid_of((128, 128))
    return ones_where(x == natural_of(y))


def spreading():
    x, y = grid_of((128, 512))
    return ones_where((x // 32 == y // 128) & (x % 32 == y % 32))


def unmixing():
    x, y = grid_of((128, 512))
    return ones_where((x // 32 == y // 128) & (natural_of(x) % 32 == y % 32))


def gathering():
    x, y = grid_of((512, 256))
    lane = y % 128
    entry = jnp.where(y < 128, lane % 32, natural_of(lane) % 32)
    return ones_where((lane // 32 == x // 128) & (entry == x % 32))


def tiling():
    x, y = grid_of((128, 128))
    return ones_where(x % 32 == y % 32)


def lane_groups(rows):
    return lax.broadcasted_iota(jnp.int32, (rows, 128), 1) // 32


def by_group(parts, group):
    out = parts[0]
    for index in range(1, len(parts)):
        out = jnp.where(group == index, parts[index], out)
    return out


def spread_rows(matrix_ref, rows, scratch):
    for first in range(0, rows, 8):
        count = min(8, rows - first)
        block = matrix_ref[first : first + count, :].astype(f32)
        for g in range(8):
            scratch[first // 8, g * 8 : g * 8 + count, :] = block[:, g * 128 : (g + 1) * 128]


def row_of(scratch, row):
    return scratch[row // 8, pl.ds(row % 8, 8, stride=8), :]


def masked_rows(rows8, group8):
    return jnp.concatenate([jnp.where(group8 == r, rows8, 0.0) for r in range(4)], axis=0)


def family(scratch, first, count, group8):
    blocks = [masked_rows(row_of(scratch, first + b), group8) for b in range(count)]
    if count < 4:
        blocks.append(jnp.zeros((32 * (4 - count), 128), f32))
    return halves(jnp.concatenate(blocks, axis=0))


def lifted(high, low, matrices):
    matrix_high, matrix_low = matrices
    return folded(dot_nn(jnp.concatenate([high, low], axis=0), matrix_high)) + dot_nn(
        high, matrix_low
    )


def lowered(coeffs, matrices):
    high, low = halves(coeffs)
    matrix_high, matrix_low = matrices
    return folded(dot_nt(jnp.concatenate([high, low], axis=0), matrix_high)) + dot_nt(
        high, matrix_low
    )


def gathered(parts, gather):
    wide = jnp.concatenate(
        parts + [jnp.zeros((NRHS, 128), f32)] * (4 - len(parts)), axis=1
    )
    both = folded(dot_nn(stacked(wide), gather))
    return both[:, :128], both[:, 128:]


def moments_kernel(density, basis, transfer, right_out, left_out, crown_out, rows):
    group16, group8 = lane_groups(16), lane_groups(8)
    spread_rows(transfer, 85, rows)
    right_out[0:HALO] = density[LEAVES - HALO : LEAVES]
    left_out[0:HALO] = density[0:HALO]
    natural = []
    for i in range(16):
        cells = density[4 * i : 4 * i + 4].reshape(64, 128)
        wide = basis[4 * i : 4 * i + 4].reshape(128, 128)
        found = folded(dot_nt(stacked(cells), wide))
        natural.append(by_group([found[16 * b : 16 * b + 16] for b in range(4)], group16))
    mix = mixing()
    gather = gathering()
    level = jnp.concatenate(natural, axis=0)
    high, low = halves(level)
    high, low = dot_nn(high, mix).astype(bf16), dot_nn(low, mix).astype(bf16)
    tile = 0
    for part in natural:
        right_out[HALO + tile] = part
        left_out[HALO + tile] = part
        tile += 1
    pairs = [(high[16 * i : 16 * i + 16], low[16 * i : 16 * i + 16]) for i in range(16)]
    for size, start in ((64, 0), (16, 64), (4, 80)):
        raised = [
            lifted(pairs[i][0], pairs[i][1], family(rows, start + 4 * i, 4, group8))
            for i in range(size // 4)
        ]
        pairs = []
        for i in range(0, size // 4, 4):
            plain, mixed = gathered(raised[i : i + 4], gather)
            right_out[HALO + tile] = plain
            left_out[HALO + tile] = plain
            tile += 1
            pairs.append(halves(mixed))
    crown = lifted(pairs[0][0], pairs[0][1], family(rows, 84, 1, group8))
    crown = folded(dot_nn(stacked(crown), tiling()))
    packed = by_group([crown[4 * b : 4 * b + 4] for b in range(4)], lane_groups(4))
    for i in range(SLOTS):
        crown_out[i] = packed


def moments_call(density, basis, transfer):
    sent = jax.ShapeDtypeStruct((HALO + TILES, NRHS, 128), f32)
    return pl.pallas_call(
        moments_kernel,
        out_shape=(sent, sent, jax.ShapeDtypeStruct((SLOTS, 4, 128), f32)),
        scratch_shapes=[pltpu.VMEM((11, 64, 128), f32)],
        compiler_params=PARAMS,
        name="moments",
    )(density, basis, transfer)


def local_kernel(
    count,
    near_rows,
    near_cols,
    sources,
    density,
    mine,
    before,
    after,
    tiles,
    coupling,
    near,
    field,
    cells,
    terms,
    rows,
    found,
):
    group8 = lane_groups(8)
    near[...] = jnp.zeros_like(near)

    def from_before(i, carry):
        for u in range(4):
            cells[i * 4 + u] = stacked(before[i * 4 + u])
            cells[HALO + LEAVES + i * 4 + u] = stacked(after[i * 4 + u])
        for u in range(8):
            cells[HALO + i * 8 + u] = stacked(density[i * 8 + u])
        return carry

    lax.fori_loop(0, 8, from_before, 0)
    live = count[0]
    step = 16

    def near_step(turn, carry):
        products = []
        for u in range(step):
            slot = turn * step + u
            product = folded(dot_nt(cells[near_cols[slot]], tiles[slot]))
            products.append(jnp.where(slot < live, product, 0.0))
        for u in range(step):
            row = near_rows[turn * step + u]
            near[row] = near[row] + products[u]
        return carry

    lax.fori_loop(0, (live + step - 1) // step, near_step, 0)

    spread = spreading()
    for place, origin in enumerate((before, mine, after)):

        def spread_terms(i, carry):
            both = stacked(origin[pl.ds(HALO + 2 * i, 2)].reshape(32, 128))
            wide = dot_nn(both, spread).astype(bf16)
            for t in range(2):
                for b in range(4):
                    lanes = slice(b * 128, (b + 1) * 128)
                    at = place * SPAN + (2 * i + t) * 4 + b
                    terms[at, 0:16] = wide[16 * t : 16 * t + 16, lanes]
                    terms[at, 16:32] = wide[32 + 16 * t : 48 + 16 * t, lanes]
            return carry

        lax.fori_loop(0, TILES // 2, spread_terms, 0)

    def couple(first, size):
        base = first if isinstance(first, int) else pl.multiple_of(first, 16)
        for j in range(FAR):
            block = coupling[j, pl.ds(base, size), :].astype(f32)
            for half in range(0, size, 8):
                count8 = min(8, size - half)
                for g in range(8):
                    rows[j, half // 8, g * 8 : g * 8 + count8, :] = block[
                        half : half + count8, g * 128 : (g + 1) * 128
                    ]
        for c in range(size):
            total = jnp.zeros((32, 32), f32)
            for j in range(0, FAR, 2):
                pair = range(j, min(j + 2, FAR))
                left = [
                    masked_rows(
                        rows[jj, c // 8, pl.ds(c % 8, 8, stride=8), :], group8
                    ).astype(bf16)
                    for jj in pair
                ]
                right = [terms[sources[first + c, jj]] for jj in pair]
                total = total + dot_nt(
                    jnp.concatenate(right, axis=1), jnp.concatenate(left, axis=1)
                )
            found[first + c] = folded(total)

    def couple_step(i, carry):
        couple(i * 16, 16)
        return carry

    lax.fori_loop(0, 5, couple_step, 0)
    couple(80, 5)
    for i in range(TILES - 1):
        field[i] = jnp.concatenate([found[4 * i + b] for b in range(4)], axis=1)
    field[TILES - 1] = jnp.concatenate([found[84], jnp.zeros((NRHS, 96), f32)], axis=1)


def local_call(count, near_rows, near_cols, sources, density, mine, before, after, tiles, coupling):
    scalar = pl.BlockSpec(memory_space=pltpu.SMEM)
    vector = pl.BlockSpec(memory_space=pltpu.VMEM)
    return pl.pallas_call(
        local_kernel,
        out_shape=(
            jax.ShapeDtypeStruct((LEAVES, NRHS, 128), f32),
            jax.ShapeDtypeStruct((TILES, NRHS, 128), f32),
        ),
        in_specs=[scalar] * 4 + [vector] * 6,
        out_specs=(vector, vector),
        scratch_shapes=[
            pltpu.VMEM((2 * HALO + LEAVES, 2 * NRHS, 128), bf16),
            pltpu.VMEM((3 * SPAN, 2 * NRHS, 128), bf16),
            pltpu.VMEM((FAR, 2, 64, 128), f32),
            pltpu.VMEM((85, NRHS, RANK), f32),
        ],
        cost_estimate=pl.CostEstimate(
            flops=2_000_000_000, bytes_accessed=40_000_000, transcendentals=0
        ),
        compiler_params=PARAMS,
        name="local",
    )(count, near_rows, near_cols, sources, density, mine, before, after, tiles, coupling)


def crown_kernel(
    place,
    sources,
    terms_in,
    couple0,
    couple1,
    couple2,
    transfer_top,
    transfer,
    basis,
    field,
    near,
    out,
    top_rows,
    own_rows,
    link_rows,
    loose,
    terms,
):
    group8, group16, group32 = lane_groups(8), lane_groups(16), lane_groups(32)
    mix, spread, gather, unmix = mixing(), spreading(), gathering(), unmixing()
    spread_rows(transfer_top, 42, top_rows)
    spread_rows(transfer, 85, own_rows)
    cells = []
    for c in range(32):
        cells.append(
            (terms_in[4 * c] + terms_in[4 * c + 1]) + (terms_in[4 * c + 2] + terms_in[4 * c + 3])
        )
    wide = dot_nn(stacked(jnp.concatenate(cells, axis=0)), spread)
    for c in range(32):
        for b in range(4):
            lanes = slice(b * 128, (b + 1) * 128)
            loose[c, 4 * b : 4 * b + 4] = wide[4 * c : 4 * c + 4, lanes]
            loose[c, 16 + 4 * b : 20 + 4 * b] = wide[128 + 4 * c : 132 + 4 * c, lanes]
    packed = []
    for i in range(8):
        for b in range(4):
            terms[4 * i + b] = loose[4 * i + b].astype(bf16)
        packed.append(by_group([loose[4 * i + b] for b in range(4)], group32).astype(bf16))
    mixed = dot_nn(jnp.concatenate(packed, axis=0), mix).astype(bf16)
    pairs = [(mixed[32 * i : 32 * i + 16], mixed[32 * i + 16 : 32 * i + 32]) for i in range(8)]
    for size, start, at in ((32, 0, 32), (8, 32, 40)):
        raised = [
            lifted(pairs[i][0], pairs[i][1], family(top_rows, start + 4 * i, 4, group8))
            for i in range(size // 4)
        ]
        pairs = []
        for i in range(0, size // 4, 4):
            plain, mixed = gathered(raised[i : i + 4], gather)
            pairs.append(halves(mixed))
            wide = dot_nn(stacked(plain), spread).astype(bf16)
            for b in range(min(4, size // 4)):
                terms[at + i + b] = wide[:, b * 128 : (b + 1) * 128]
    fields = []
    for level, link in enumerate((couple0, couple1, couple2)):
        for first in (0, 16):
            block = link[0, first : min(first + 16, FAR), :].astype(f32)
            for half in (0, 8):
                count = min(8, FAR - first - half)
                for g in range(8):
                    link_rows[level, (first + half) // 8, g * 8 : g * 8 + count, :] = block[
                        half : half + count, g * 128 : (g + 1) * 128
                    ]
        total = jnp.zeros((32, 32), f32)
        for j in range(0, FAR, 2):
            pair = range(j, min(j + 2, FAR))
            left = [
                masked_rows(
                    link_rows[level, jj // 8, pl.ds(jj % 8, 8, stride=8), :], group8
                ).astype(bf16)
                for jj in pair
            ]
            right = [
                terms[UPPER_STARTS[level] + sources[UPPER_STARTS[level] + place[level], jj]]
                for jj in pair
            ]
            total = total + dot_nt(jnp.concatenate(right, axis=1), jnp.concatenate(left, axis=1))
        fields.append(folded(total))

    def one_tiled(mixed):
        padded = jnp.concatenate([mixed, jnp.zeros((NRHS, 96), f32)], axis=1)
        return folded(dot_nn(stacked(padded), unmix[:, 0:128]))

    def top_family(index):
        rows8 = top_rows[index // 8, pl.ds(index % 8, 8, stride=8), :]
        return halves(masked_rows(rows8, group8))

    coeffs = one_tiled(fields[2])
    coeffs = one_tiled(fields[1] + lowered(coeffs, top_family(UPPER_STARTS[1] + place[1])))
    coeffs = one_tiled(fields[0] + lowered(coeffs, top_family(UPPER_STARTS[0] + place[0])))
    parents = [coeffs]
    tile = TILES - 1
    for size, start in ((1, 84), (4, 80), (16, 64), (64, 0)):
        tiles_here = (size + 3) // 4
        first = tile - tiles_here + 1
        children = []
        for i in range(tiles_here):
            matrices = family(own_rows, start + 4 * i, min(4, size), group8)
            mixed = field[first + i] + lowered(parents[i], matrices)
            wide = folded(dot_nn(stacked(mixed), unmix))
            children += [wide[:, b * 128 : (b + 1) * 128] for b in range(min(4, size))]
        parents = children
        tile = first - 1
    for i in range(16):
        blocks = [jnp.where(group16 == b, parents[4 * i + b], 0.0) for b in range(4)]
        far = folded(
            dot_nn(
                stacked(jnp.concatenate(blocks, axis=0)),
                basis[4 * i : 4 * i + 4].reshape(128, 128),
            )
        )
        out[4 * i : 4 * i + 4] = near[4 * i : 4 * i + 4] + far.reshape(4, NRHS, 128)


def crown_call(place, sources, terms, coupling_top, transfer_top, transfer, basis, field, near):
    def whole(array):
        return pl.BlockSpec(array.shape, lambda i, place, sources: (0,) * array.ndim)

    def link(level):
        return pl.BlockSpec(
            (1, FAR, RANK * RANK),
            lambda i, place, sources: (UPPER_STARTS[level] + place[level], 0, 0),
        )

    return pl.pallas_call(
        crown_kernel,
        grid_spec=pltpu.PrefetchScalarGridSpec(
            num_scalar_prefetch=2,
            grid=(1,),
            in_specs=[whole(terms), link(0), link(1), link(2)]
            + [whole(array) for array in (transfer_top, transfer, basis, field, near)],
            out_specs=pl.BlockSpec(
                (LEAVES, NRHS, 128), lambda i, place, sources: (0, 0, 0)
            ),
            scratch_shapes=[
                pltpu.VMEM((6, 64, 128), f32),
                pltpu.VMEM((11, 64, 128), f32),
                pltpu.VMEM((3, 4, 64, 128), f32),
                pltpu.VMEM((32, 32, 128), f32),
                pltpu.VMEM((42, 32, 128), bf16),
            ],
        ),
        out_shape=jax.ShapeDtypeStruct((LEAVES, NRHS, 128), f32),
        compiler_params=PARAMS,
        name="crown",
    )(
        place,
        sources,
        terms,
        coupling_top,
        coupling_top,
        coupling_top,
        transfer_top,
        transfer,
        basis,
        field,
        near,
    )


def body(
    density,
    leaf_basis,
    near_tiles,
    near_rows,
    near_cols,
    near_count,
    far_src,
    coupling,
    transfer,
    far_src_top,
    coupling_top,
    transfer_top,
):
    devices = lax.axis_size("leaf") * lax.axis_size("sub")
    device = lax.axis_index(AXES)
    right, left, crown = moments_call(density, leaf_basis, transfer)
    before = lax.ppermute(right, AXES, [(i, i + 1) for i in range(devices - 1)])
    after = lax.ppermute(left, AXES, [(i + 1, i) for i in range(devices - 1)])
    terms = lax.all_to_all(crown, AXES, 0, 0, tiled=True)

    cluster = jnp.arange(85, dtype=jnp.int32)[:, None]
    shift = jnp.where(cluster < 64, 6, jnp.where(cluster < 80, 4, jnp.where(cluster < 84, 2, 0)))
    start = jnp.where(cluster < 64, 0, jnp.where(cluster < 80, 64, jnp.where(cluster < 84, 80, 84)))
    owner = (far_src >> shift) - (device - 1)
    within = far_src & ((1 << shift) - 1)
    sources = owner * SPAN + start + within

    near, field = local_call(
        near_count,
        near_rows - device * LEAVES,
        near_cols - (device * LEAVES - HALO),
        sources,
        density,
        right,
        before,
        after,
        near_tiles,
        coupling,
    )
    place = jnp.stack([device // 4, device // 16, device // 64]).astype(jnp.int32)
    return crown_call(
        place,
        far_src_top,
        terms,
        coupling_top,
        transfer_top,
        transfer,
        leaf_basis,
        field,
        near,
    )


def solution(mesh):
    placed = (
        P(AXES, None, None),
        P(AXES, None, None),
        P(AXES, None, None),
        P(AXES),
        P(AXES),
        P(AXES),
        P(AXES, None),
        P(None, AXES, None),
        P(AXES, None),
        P(),
        P(),
        P(),
    )
    return jax.shard_map(
        body, mesh=mesh, in_specs=placed, out_specs=P(AXES, None, None), check_vma=False
    )
```

```python
import jax
import jax.numpy as jnp
from jax import lax
from jax.experimental import pallas as pl
from jax.experimental.pallas import tpu as pltpu
from jax.sharding import PartitionSpec as P

f32, bf16 = jnp.float32, jnp.bfloat16
AXES = ("leaf", "sub")
LEAVES = 64
HALO = 32
NRHS = 16
RANK = 32
FAR = 27
SLOTS = 128
LEVELS = (64, 16, 4, 1)
STARTS = (0, 64, 80, 84)
UPPER = (32, 8, 2)
UPPER_STARTS = (0, 32, 40)
TILES = 22
SPAN = 4 * TILES
LOCAL_FLOPS = 2_000_000_000
PARAMS = pltpu.CompilerParams(vmem_limit_bytes=60 * 1024 * 1024)


def dot_nn(a, b):
    return lax.dot_general(a, b, (((1,), (0,)), ((), ())), preferred_element_type=f32)


def dot_nt(a, b):
    return lax.dot_general(a, b, (((1,), (1,)), ((), ())), preferred_element_type=f32)


def halves(x):
    high = x.astype(bf16)
    return high, (x - high.astype(f32)).astype(bf16)


def stacked(x):
    high, low = halves(x)
    return jnp.concatenate([high, low], axis=0)


def folded(x):
    half = x.shape[0] // 2
    return x[:half] + x[half:]


def grid_of(shape):
    return (
        lax.broadcasted_iota(jnp.int32, shape, 0),
        lax.broadcasted_iota(jnp.int32, shape, 1),
    )


def ones_where(mask):
    return jnp.where(mask, 1.0, 0.0).astype(bf16)


def natural_of(lane):
    return (lane // 32) * 32 + 4 * (lane % 8) + (lane % 32) // 8


def mixing():
    x, y = grid_of((128, 128))
    return ones_where(x == natural_of(y))


def spreading():
    x, y = grid_of((128, 512))
    return ones_where((x // 32 == y // 128) & (x % 32 == y % 32))


def unmixing():
    x, y = grid_of((128, 512))
    return ones_where((x // 32 == y // 128) & (natural_of(x) % 32 == y % 32))


def gathering():
    x, y = grid_of((512, 256))
    lane = y % 128
    entry = jnp.where(y < 128, lane % 32, natural_of(lane) % 32)
    return ones_where((lane // 32 == x // 128) & (entry == x % 32))


def tiling():
    x, y = grid_of((128, 128))
    return ones_where(x % 32 == y % 32)


def lane_groups(rows):
    return lax.broadcasted_iota(jnp.int32, (rows, 128), 1) // 32


def by_group(parts, group):
    out = parts[0]
    for index in range(1, len(parts)):
        out = jnp.where(group == index, parts[index], out)
    return out


def spread_rows(matrix_ref, rows, scratch):
    for first in range(0, rows, 8):
        count = min(8, rows - first)
        block = matrix_ref[first : first + count, :].astype(f32)
        for g in range(8):
            scratch[first // 8, g * 8 : g * 8 + count, :] = block[:, g * 128 : (g + 1) * 128]


def row_of(scratch, row):
    return scratch[row // 8, pl.ds(row % 8, 8, stride=8), :]


def masked_rows(rows8, group8):
    return jnp.concatenate([jnp.where(group8 == r, rows8, 0.0) for r in range(4)], axis=0)


def family(scratch, first, count, group8):
    blocks = [masked_rows(row_of(scratch, first + b), group8) for b in range(count)]
    if count < 4:
        blocks.append(jnp.zeros((32 * (4 - count), 128), f32))
    return halves(jnp.concatenate(blocks, axis=0))


def lifted(high, low, matrices):
    matrix_high, matrix_low = matrices
    return folded(dot_nn(jnp.concatenate([high, low], axis=0), matrix_high)) + dot_nn(
        high, matrix_low
    )


def lowered(coeffs, matrices):
    high, low = halves(coeffs)
    matrix_high, matrix_low = matrices
    return folded(dot_nt(jnp.concatenate([high, low], axis=0), matrix_high)) + dot_nt(
        high, matrix_low
    )


def gathered(parts, gather):
    wide = jnp.concatenate(
        parts + [jnp.zeros((NRHS, 128), f32)] * (4 - len(parts)), axis=1
    )
    both = folded(dot_nn(stacked(wide), gather))
    return both[:, :128], both[:, 128:]


def own_index():
    return lax.axis_index("leaf") * lax.axis_size("sub") + lax.axis_index("sub")


def start_copies(pairs, semaphores):
    copies = [
        pltpu.make_async_copy(source, target, semaphores.at[i])
        for i, (source, target) in enumerate(pairs)
    ]
    for copy in copies:
        copy.start()
    return copies


def moments_kernel(
    density_in,
    basis_in,
    transfer_in,
    right_out,
    left_out,
    crown_out,
    density,
    basis,
    transfer,
    rows,
    summed,
    crown_terms,
    semaphores,
):
    copies = start_copies(
        [
            (density_in, density),
            (basis_in, basis),
            (transfer_in, transfer),
        ],
        semaphores,
    )
    group16, group8 = lane_groups(16), lane_groups(8)
    mix = mixing()
    gather = gathering()
    copies[0].wait()
    for i, (target, first) in enumerate(((right_out, LEAVES - HALO), (left_out, 0))):
        copy = pltpu.make_async_copy(
            density.at[pl.ds(first, HALO)], target.at[pl.ds(0, HALO)], semaphores.at[3 + i]
        )
        copy.start()
        copies.append(copy)
    copies[1].wait()
    natural = []
    for i in range(16):
        cells = density[4 * i : 4 * i + 4].reshape(64, 128)
        wide = basis[4 * i : 4 * i + 4].reshape(128, 128)
        found = folded(dot_nt(stacked(cells), wide))
        natural.append(by_group([found[16 * b : 16 * b + 16] for b in range(4)], group16))
    level = jnp.concatenate(natural, axis=0)
    high, low = halves(level)
    high, low = dot_nn(high, mix).astype(bf16), dot_nn(low, mix).astype(bf16)
    tile = 0
    for part in natural:
        summed[tile] = part
        tile += 1
    copies[2].wait()
    spread_rows(transfer, 85, rows)
    pairs = [(high[16 * i : 16 * i + 16], low[16 * i : 16 * i + 16]) for i in range(16)]
    for size, start in ((64, 0), (16, 64), (4, 80)):
        raised = [
            lifted(pairs[i][0], pairs[i][1], family(rows, start + 4 * i, 4, group8))
            for i in range(size // 4)
        ]
        pairs = []
        for i in range(0, size // 4, 4):
            plain, mixed = gathered(raised[i : i + 4], gather)
            summed[tile] = plain
            tile += 1
            pairs.append(halves(mixed))
    for i, target in enumerate((right_out, left_out)):
        copy = pltpu.make_async_copy(
            summed, target.at[pl.ds(HALO, TILES)], semaphores.at[5 + i]
        )
        copy.start()
        copies.append(copy)
    crown = lifted(pairs[0][0], pairs[0][1], family(rows, 84, 1, group8))
    crown = folded(dot_nn(stacked(crown), tiling()))
    packed = by_group([crown[4 * b : 4 * b + 4] for b in range(4)], lane_groups(4))
    for i in range(SLOTS):
        crown_terms[i] = packed
    last = pltpu.make_async_copy(crown_terms, crown_out, semaphores.at[7])
    last.start()
    for copy in copies[3:] + [last]:
        copy.wait()


HBM = pl.BlockSpec(memory_space=pltpu.HBM)
VMEM = pl.BlockSpec(memory_space=pltpu.VMEM)
SMEM = pl.BlockSpec(memory_space=pltpu.SMEM)


def moments_call(density, basis, transfer):
    sent = jax.ShapeDtypeStruct((HALO + TILES, NRHS, 128), f32)
    return pl.pallas_call(
        moments_kernel,
        out_shape=(sent, sent, jax.ShapeDtypeStruct((SLOTS, 4, 128), f32)),
        in_specs=[HBM] * 3,
        out_specs=(HBM,) * 3,
        scratch_shapes=[
            pltpu.VMEM((LEAVES, NRHS, 128), f32),
            pltpu.VMEM((LEAVES, RANK, 128), bf16),
            pltpu.VMEM((85, RANK * RANK), f32),
            pltpu.VMEM((11, 64, 128), f32),
            pltpu.VMEM((TILES, NRHS, 128), f32),
            pltpu.VMEM((SLOTS, 4, 128), f32),
            pltpu.SemaphoreType.DMA((8,)),
        ],
        compiler_params=PARAMS,
        name="moments",
    )(density, basis, transfer)


def local_kernel(
    count,
    near_rows,
    near_cols,
    far_src,
    density_in,
    mine_in,
    before_in,
    after_in,
    tiles_in,
    coupling_in,
    near_out,
    field_out,
    near,
    field,
    density,
    mine,
    before,
    after,
    tiles,
    coupling,
    cells,
    terms,
    rows,
    found,
    places,
    sources,
    semaphores,
    tile_semaphores,
):
    live = count[0]
    step = 16
    turns = (live + step - 1) // step
    device = own_index()
    copies = start_copies(
        [(density_in, density), (before_in, before), (after_in, after), (mine_in, mine)],
        semaphores,
    )

    def tile_copy(turn):
        part = pl.ds(turn * step, step)
        return pltpu.make_async_copy(tiles_in.at[part], tiles.at[part], tile_semaphores.at[turn])

    for turn in range(SLOTS // step):

        @pl.when(turn < turns)
        def _():
            tile_copy(turn).start()

    link_copy = pltpu.make_async_copy(coupling_in, coupling, semaphores.at[4])
    link_copy.start()

    cluster = lax.broadcasted_iota(jnp.int32, (FAR, 85), 1)

    def per_level(values):
        return jnp.where(
            cluster < 64,
            values[0],
            jnp.where(cluster < 80, values[1], jnp.where(cluster < 84, values[2], values[3])),
        )

    named = far_src[...]
    owner = lax.shift_right_logical(named, per_level((6, 4, 2, 0))) - (device - 1)
    within = named & per_level((63, 15, 3, 0))
    places[...] = owner * SPAN + per_level(STARTS) + within
    place_copy = pltpu.make_async_copy(places, sources, semaphores.at[5])
    place_copy.start()

    group8 = lane_groups(8)
    near[...] = jnp.zeros_like(near)
    for copy in copies:
        copy.wait()

    def fill_cells(i, carry):
        for u in range(4):
            cells[i * 4 + u] = stacked(before[i * 4 + u])
            cells[HALO + LEAVES + i * 4 + u] = stacked(after[i * 4 + u])
        for u in range(8):
            cells[HALO + i * 8 + u] = stacked(density[i * 8 + u])
        return carry

    lax.fori_loop(0, 8, fill_cells, 0)

    spread = spreading()
    for place, origin in enumerate((before, mine, after)):

        def spread_terms(i, carry):
            both = stacked(origin[pl.ds(HALO + 2 * i, 2)].reshape(32, 128))
            wide = dot_nn(both, spread).astype(bf16)
            for t in range(2):
                for b in range(4):
                    lanes = slice(b * 128, (b + 1) * 128)
                    at = place * SPAN + (2 * i + t) * 4 + b
                    terms[at, 0:16] = wide[16 * t : 16 * t + 16, lanes]
                    terms[at, 16:32] = wide[32 + 16 * t : 48 + 16 * t, lanes]
            return carry

        lax.fori_loop(0, TILES // 2, spread_terms, 0)

    first_row = device * LEAVES
    first_col = first_row - HALO

    def near_step(turn, carry):
        tile_copy(turn).wait()
        products = []
        for u in range(step):
            slot = turn * step + u
            product = folded(dot_nt(cells[near_cols[slot] - first_col], tiles[slot]))
            products.append(jnp.where(slot < live, product, 0.0))
        for u in range(step):
            row = near_rows[turn * step + u] - first_row
            near[row] = near[row] + products[u]
        return carry

    lax.fori_loop(0, turns, near_step, 0)
    near_copy = pltpu.make_async_copy(near, near_out, semaphores.at[6])
    near_copy.start()
    place_copy.wait()
    link_copy.wait()

    def couple(first, size):
        base = first if isinstance(first, int) else pl.multiple_of(first, 16)
        for j in range(FAR):
            block = coupling[j, pl.ds(base, size), :].astype(f32)
            for half in range(0, size, 8):
                count8 = min(8, size - half)
                for g in range(8):
                    rows[j, half // 8, g * 8 : g * 8 + count8, :] = block[
                        half : half + count8, g * 128 : (g + 1) * 128
                    ]
        for c in range(size):
            total = jnp.zeros((32, 32), f32)
            for j in range(0, FAR, 2):
                pair = range(j, min(j + 2, FAR))
                left = [
                    masked_rows(
                        rows[jj, c // 8, pl.ds(c % 8, 8, stride=8), :], group8
                    ).astype(bf16)
                    for jj in pair
                ]
                right = [terms[sources[jj, first + c]] for jj in pair]
                total = total + dot_nt(
                    jnp.concatenate(right, axis=1), jnp.concatenate(left, axis=1)
                )
            found[first + c] = folded(total)

    def couple_step(i, carry):
        couple(i * 16, 16)
        return carry

    lax.fori_loop(0, 5, couple_step, 0)
    couple(80, 5)
    for i in range(TILES - 1):
        field[i] = jnp.concatenate([found[4 * i + b] for b in range(4)], axis=1)
    field[TILES - 1] = jnp.concatenate([found[84], jnp.zeros((NRHS, 96), f32)], axis=1)
    field_copy = pltpu.make_async_copy(field, field_out, semaphores.at[7])
    field_copy.start()
    near_copy.wait()
    field_copy.wait()


def local_call(count, near_rows, near_cols, far_src, density, mine, before, after, tiles, coupling):
    sent = pltpu.VMEM((HALO + TILES, NRHS, 128), f32)
    return pl.pallas_call(
        local_kernel,
        out_shape=(
            jax.ShapeDtypeStruct((LEAVES, NRHS, 128), f32),
            jax.ShapeDtypeStruct((TILES, NRHS, 128), f32),
        ),
        in_specs=[SMEM] * 3 + [VMEM] + [HBM] * 6,
        out_specs=(HBM, HBM),
        scratch_shapes=[
            pltpu.VMEM((LEAVES, NRHS, 128), f32),
            pltpu.VMEM((TILES, NRHS, 128), f32),
            pltpu.VMEM((LEAVES, NRHS, 128), f32),
            sent,
            sent,
            sent,
            pltpu.VMEM((SLOTS, 128, 128), bf16),
            pltpu.VMEM((FAR, 85, RANK * RANK), bf16),
            pltpu.VMEM((2 * HALO + LEAVES, 2 * NRHS, 128), bf16),
            pltpu.VMEM((3 * SPAN, 2 * NRHS, 128), bf16),
            pltpu.VMEM((FAR, 2, 64, 128), f32),
            pltpu.VMEM((85, NRHS, RANK), f32),
            pltpu.VMEM((FAR, 85), jnp.int32),
            pltpu.SMEM((FAR, 85), jnp.int32),
            pltpu.SemaphoreType.DMA((8,)),
            pltpu.SemaphoreType.DMA((8,)),
        ],
        cost_estimate=pl.CostEstimate(
            flops=LOCAL_FLOPS, bytes_accessed=40_000_000, transcendentals=0
        ),
        compiler_params=PARAMS,
        name="local",
    )(count, near_rows, near_cols, far_src, density, mine, before, after, tiles, coupling)


def crown_kernel(
    sources,
    terms_in,
    field_in,
    near_in,
    coupling_in,
    transfer_top_in,
    transfer_in,
    basis_in,
    out_hbm,
    out,
    given,
    field,
    near,
    coupling,
    transfer_top,
    transfer,
    basis,
    top_rows,
    own_rows,
    link_rows,
    loose,
    terms,
    semaphores,
):
    copies = start_copies(
        [
            (transfer_top_in, transfer_top),
            (coupling_in, coupling),
            (transfer_in, transfer),
            (basis_in, basis),
            (terms_in, given),
            (field_in, field),
            (near_in, near),
        ],
        semaphores,
    )
    device = own_index()
    place = (device // 4, device // 16, device // 64)
    group8, group16, group32 = lane_groups(8), lane_groups(16), lane_groups(32)
    mix, spread, gather, unmix = mixing(), spreading(), gathering(), unmixing()
    copies[0].wait()
    spread_rows(transfer_top, 42, top_rows)
    copies[4].wait()
    cells = []
    for c in range(32):
        cells.append((given[4 * c] + given[4 * c + 1]) + (given[4 * c + 2] + given[4 * c + 3]))
    wide = dot_nn(stacked(jnp.concatenate(cells, axis=0)), spread)
    for c in range(32):
        for b in range(4):
            lanes = slice(b * 128, (b + 1) * 128)
            loose[c, 4 * b : 4 * b + 4] = wide[4 * c : 4 * c + 4, lanes]
            loose[c, 16 + 4 * b : 20 + 4 * b] = wide[128 + 4 * c : 132 + 4 * c, lanes]
    packed = []
    for i in range(8):
        for b in range(4):
            terms[4 * i + b] = loose[4 * i + b].astype(bf16)
        packed.append(by_group([loose[4 * i + b] for b in range(4)], group32).astype(bf16))
    mixed = dot_nn(jnp.concatenate(packed, axis=0), mix).astype(bf16)
    pairs = [(mixed[32 * i : 32 * i + 16], mixed[32 * i + 16 : 32 * i + 32]) for i in range(8)]
    for size, start, at in ((32, 0, 32), (8, 32, 40)):
        raised = [
            lifted(pairs[i][0], pairs[i][1], family(top_rows, start + 4 * i, 4, group8))
            for i in range(size // 4)
        ]
        pairs = []
        for i in range(0, size // 4, 4):
            plain, mixed = gathered(raised[i : i + 4], gather)
            pairs.append(halves(mixed))
            wide = dot_nn(stacked(plain), spread).astype(bf16)
            for b in range(min(4, size // 4)):
                terms[at + i + b] = wide[:, b * 128 : (b + 1) * 128]
    copies[1].wait()
    half = pl.multiple_of((place[0] // 16) * 16, 16)
    upper8 = (place[0] % 16) < 8
    for j in range(FAR):
        block = coupling[j, pl.ds(half, 16), :].astype(f32)
        block = jnp.where(upper8, block[0:8], block[8:16])
        last = coupling[j, 32:42, :].astype(f32)
        for g in range(8):
            lanes = slice(g * 128, (g + 1) * 128)
            link_rows[0, j, g * 8 : g * 8 + 8, :] = block[:, lanes]
            link_rows[1, j, g * 8 : g * 8 + 8, :] = last[0:8, lanes]
            link_rows[2, j, g * 8 : g * 8 + 2, :] = last[8:10, lanes]
    fields = []
    for level in range(3):
        total = jnp.zeros((32, 32), f32)
        for j in range(0, FAR, 2):
            pair = range(j, min(j + 2, FAR))
            left = [
                masked_rows(
                    link_rows[level, jj, pl.ds(place[level] % 8, 8, stride=8), :], group8
                ).astype(bf16)
                for jj in pair
            ]
            right = [
                terms[UPPER_STARTS[level] + sources[jj, UPPER_STARTS[level] + place[level]]]
                for jj in pair
            ]
            total = total + dot_nt(jnp.concatenate(right, axis=1), jnp.concatenate(left, axis=1))
        fields.append(folded(total))

    def one_tiled(mixed):
        padded = jnp.concatenate([mixed, jnp.zeros((NRHS, 96), f32)], axis=1)
        return folded(dot_nn(stacked(padded), unmix[:, 0:128]))

    def top_family(index):
        rows8 = top_rows[index // 8, pl.ds(index % 8, 8, stride=8), :]
        return halves(masked_rows(rows8, group8))

    coeffs = one_tiled(fields[2])
    coeffs = one_tiled(fields[1] + lowered(coeffs, top_family(UPPER_STARTS[1] + place[1])))
    coeffs = one_tiled(fields[0] + lowered(coeffs, top_family(UPPER_STARTS[0] + place[0])))
    copies[2].wait()
    spread_rows(transfer, 85, own_rows)
    copies[5].wait()
    parents = [coeffs]
    tile = TILES - 1
    for size, start in ((1, 84), (4, 80), (16, 64), (64, 0)):
        tiles_here = (size + 3) // 4
        first = tile - tiles_here + 1
        children = []
        for i in range(tiles_here):
            matrices = family(own_rows, start + 4 * i, min(4, size), group8)
            mixed = field[first + i] + lowered(parents[i], matrices)
            wide = folded(dot_nn(stacked(mixed), unmix))
            children += [wide[:, b * 128 : (b + 1) * 128] for b in range(min(4, size))]
        parents = children
        tile = first - 1
    copies[3].wait()
    copies[6].wait()
    sent = []
    for i in range(16):
        blocks = [jnp.where(group16 == b, parents[4 * i + b], 0.0) for b in range(4)]
        far = folded(
            dot_nn(
                stacked(jnp.concatenate(blocks, axis=0)),
                basis[4 * i : 4 * i + 4].reshape(128, 128),
            )
        )
        out[4 * i : 4 * i + 4] = near[4 * i : 4 * i + 4] + far.reshape(4, NRHS, 128)
        if i % 4 == 3:
            part = pl.ds(4 * i - 12, 16)
            sent.append(
                pltpu.make_async_copy(out.at[part], out_hbm.at[part], semaphores.at[7 + i // 4])
            )
            sent[-1].start()
    for copy in sent:
        copy.wait()


def crown_call(sources, terms, field, near, coupling_top, transfer_top, transfer, basis):
    return pl.pallas_call(
        crown_kernel,
        out_shape=jax.ShapeDtypeStruct((LEAVES, NRHS, 128), f32),
        in_specs=[SMEM] + [HBM] * 7,
        out_specs=HBM,
        scratch_shapes=[
            pltpu.VMEM((LEAVES, NRHS, 128), f32),
            pltpu.VMEM((SLOTS, 4, 128), f32),
            pltpu.VMEM((TILES, NRHS, 128), f32),
            pltpu.VMEM((LEAVES, NRHS, 128), f32),
            pltpu.VMEM((FAR, 42, RANK * RANK), bf16),
            pltpu.VMEM((42, RANK * RANK), f32),
            pltpu.VMEM((85, RANK * RANK), f32),
            pltpu.VMEM((LEAVES, RANK, 128), bf16),
            pltpu.VMEM((6, 64, 128), f32),
            pltpu.VMEM((11, 64, 128), f32),
            pltpu.VMEM((3, FAR, 64, 128), f32),
            pltpu.VMEM((32, 32, 128), f32),
            pltpu.VMEM((42, 32, 128), bf16),
            pltpu.SemaphoreType.DMA((11,)),
        ],
        compiler_params=PARAMS,
        name="crown",
    )(sources, terms, field, near, coupling_top, transfer_top, transfer, basis)


def body(
    density,
    leaf_basis,
    near_tiles,
    near_rows,
    near_cols,
    near_count,
    far_src,
    coupling,
    transfer,
    far_src_top,
    coupling_top,
    transfer_top,
):
    devices = lax.axis_size("leaf") * lax.axis_size("sub")
    right, left, crown = moments_call(density, leaf_basis, transfer)
    before = lax.ppermute(right, AXES, [(i, i + 1) for i in range(devices - 1)])
    after = lax.ppermute(left, AXES, [(i + 1, i) for i in range(devices - 1)])
    terms = lax.all_to_all(crown, AXES, 0, 0, tiled=True)
    near, field = local_call(
        near_count,
        near_rows,
        near_cols,
        far_src.T,
        density,
        right,
        before,
        after,
        near_tiles,
        coupling,
    )
    return crown_call(
        far_src_top.T,
        terms,
        field,
        near,
        jnp.transpose(coupling_top, (1, 0, 2)),
        transfer_top,
        transfer,
        leaf_basis,
    )


def solution(mesh):
    placed = (
        P(AXES, None, None),
        P(AXES, None, None),
        P(AXES, None, None),
        P(AXES),
        P(AXES),
        P(AXES),
        P(AXES, None),
        P(None, AXES, None),
        P(AXES, None),
        P(),
        P(),
        P(),
    )
    return jax.shard_map(
        body, mesh=mesh, in_specs=placed, out_specs=P(AXES, None, None), check_vma=False
    )
```

```python
import jax
import jax.numpy as jnp
from jax import lax
from jax.experimental import pallas as pl
from jax.experimental.pallas import tpu as pltpu
from jax.sharding import PartitionSpec as P

f32, bf16 = jnp.float32, jnp.bfloat16
AXES = ("leaf", "sub")
LEAVES = 64
HALO = 32
NRHS = 16
RANK = 32
FAR = 27
SLOTS = 128
LEVELS = (64, 16, 4, 1)
STARTS = (0, 64, 80, 84)
UPPER = (32, 8, 2)
UPPER_STARTS = (0, 32, 40)
TILES = 22
SPAN = 4 * TILES
LOCAL_FLOPS = 2_000_000_000
PARAMS = pltpu.CompilerParams(vmem_limit_bytes=60 * 1024 * 1024)


def dot_nn(a, b):
    return lax.dot_general(a, b, (((1,), (0,)), ((), ())), preferred_element_type=f32)


def dot_nt(a, b):
    return lax.dot_general(a, b, (((1,), (1,)), ((), ())), preferred_element_type=f32)


def halves(x):
    high = x.astype(bf16)
    return high, (x - high.astype(f32)).astype(bf16)


def stacked(x):
    high, low = halves(x)
    return jnp.concatenate([high, low], axis=0)


def folded(x):
    half = x.shape[0] // 2
    return x[:half] + x[half:]


def grid_of(shape):
    return (
        lax.broadcasted_iota(jnp.int32, shape, 0),
        lax.broadcasted_iota(jnp.int32, shape, 1),
    )


def ones_where(mask):
    return jnp.where(mask, 1.0, 0.0).astype(bf16)


def natural_of(lane):
    return (lane // 32) * 32 + 4 * (lane % 8) + (lane % 32) // 8


def mixing():
    x, y = grid_of((128, 128))
    return ones_where(x == natural_of(y))


def spreading():
    x, y = grid_of((128, 512))
    return ones_where((x // 32 == y // 128) & (x % 32 == y % 32))


def unmixing():
    x, y = grid_of((128, 512))
    return ones_where((x // 32 == y // 128) & (natural_of(x) % 32 == y % 32))


def unmixing_one():
    x, y = grid_of((128, 128))
    return ones_where(y == natural_of(x))


def gathering():
    x, y = grid_of((512, 256))
    lane = y % 128
    entry = jnp.where(y < 128, lane % 32, natural_of(lane) % 32)
    return ones_where((lane // 32 == x // 128) & (entry == x % 32))


def tiling():
    x, y = grid_of((128, 128))
    return ones_where(x % 32 == y % 32)


def lane_groups(rows):
    return lax.broadcasted_iota(jnp.int32, (rows, 128), 1) // 32


def by_group(parts, group):
    out = parts[0]
    for index in range(1, len(parts)):
        out = jnp.where(group == index, parts[index], out)
    return out


def spread_rows(matrix_ref, rows, scratch):
    for first in range(0, rows, 8):
        count = min(8, rows - first)
        block = matrix_ref[first : first + count, :].astype(f32)
        for g in range(8):
            scratch[first // 8, g * 8 : g * 8 + count, :] = block[:, g * 128 : (g + 1) * 128]


def row_of(scratch, row):
    return scratch[row // 8, pl.ds(row % 8, 8, stride=8), :]


def masked_rows(rows8, group8):
    return jnp.concatenate([jnp.where(group8 == r, rows8, 0.0) for r in range(4)], axis=0)


def family(scratch, first, count, group8):
    blocks = [masked_rows(row_of(scratch, first + b), group8) for b in range(count)]
    if count < 4:
        blocks.append(jnp.zeros((32 * (4 - count), 128), f32))
    return halves(jnp.concatenate(blocks, axis=0))


def lifted(high, low, matrices):
    matrix_high, matrix_low = matrices
    return folded(dot_nn(jnp.concatenate([high, low], axis=0), matrix_high)) + dot_nn(
        high, matrix_low
    )


def lowered(coeffs, matrices):
    high, low = halves(coeffs)
    matrix_high, matrix_low = matrices
    return folded(dot_nt(jnp.concatenate([high, low], axis=0), matrix_high)) + dot_nt(
        high, matrix_low
    )


def gathered(parts, gather):
    wide = jnp.concatenate(
        parts + [jnp.zeros((NRHS, 128), f32)] * (4 - len(parts)), axis=1
    )
    both = folded(dot_nn(stacked(wide), gather))
    return both[:, :128], both[:, 128:]


def own_index():
    return lax.axis_index("leaf") * lax.axis_size("sub") + lax.axis_index("sub")


def start_copies(pairs, semaphores):
    copies = [
        pltpu.make_async_copy(source, target, semaphores.at[i])
        for i, (source, target) in enumerate(pairs)
    ]
    for copy in copies:
        copy.start()
    return copies


def moments_kernel(
    density_in,
    basis_in,
    transfer_in,
    right_out,
    left_out,
    crown_out,
    density,
    basis,
    transfer,
    rows,
    summed,
    crown_terms,
    semaphores,
):
    copies = start_copies(
        [
            (density_in, density),
            (basis_in, basis),
            (transfer_in, transfer),
        ],
        semaphores,
    )
    group16, group8 = lane_groups(16), lane_groups(8)
    mix = mixing()
    gather = gathering()
    copies[0].wait()
    for i, (target, first) in enumerate(((right_out, LEAVES - HALO), (left_out, 0))):
        copy = pltpu.make_async_copy(
            density.at[pl.ds(first, HALO)], target.at[pl.ds(0, HALO)], semaphores.at[3 + i]
        )
        copy.start()
        copies.append(copy)
    copies[1].wait()
    natural = []
    for i in range(16):
        cells = density[4 * i : 4 * i + 4].reshape(64, 128)
        wide = basis[4 * i : 4 * i + 4].reshape(128, 128)
        found = folded(dot_nt(stacked(cells), wide))
        natural.append(by_group([found[16 * b : 16 * b + 16] for b in range(4)], group16))
    level = jnp.concatenate(natural, axis=0)
    high, low = halves(level)
    high, low = dot_nn(high, mix).astype(bf16), dot_nn(low, mix).astype(bf16)
    tile = 0
    for part in natural:
        summed[tile] = part
        tile += 1
    copies[2].wait()
    spread_rows(transfer, 85, rows)
    pairs = [(high[16 * i : 16 * i + 16], low[16 * i : 16 * i + 16]) for i in range(16)]
    for size, start in ((64, 0), (16, 64), (4, 80)):
        raised = [
            lifted(pairs[i][0], pairs[i][1], family(rows, start + 4 * i, 4, group8))
            for i in range(size // 4)
        ]
        pairs = []
        for i in range(0, size // 4, 4):
            plain, mixed = gathered(raised[i : i + 4], gather)
            summed[tile] = plain
            tile += 1
            pairs.append(halves(mixed))
    for i, target in enumerate((right_out, left_out)):
        copy = pltpu.make_async_copy(
            summed, target.at[pl.ds(HALO, TILES)], semaphores.at[5 + i]
        )
        copy.start()
        copies.append(copy)
    crown = lifted(pairs[0][0], pairs[0][1], family(rows, 84, 1, group8))
    crown = folded(dot_nn(stacked(crown), tiling()))
    packed = by_group([crown[4 * b : 4 * b + 4] for b in range(4)], lane_groups(4))
    for i in range(SLOTS):
        crown_terms[i] = packed
    last = pltpu.make_async_copy(crown_terms, crown_out, semaphores.at[7])
    last.start()
    for copy in copies[3:] + [last]:
        copy.wait()


HBM = pl.BlockSpec(memory_space=pltpu.HBM)
VMEM = pl.BlockSpec(memory_space=pltpu.VMEM)
SMEM = pl.BlockSpec(memory_space=pltpu.SMEM)


def moments_call(density, basis, transfer):
    sent = jax.ShapeDtypeStruct((HALO + TILES, NRHS, 128), f32)
    return pl.pallas_call(
        moments_kernel,
        out_shape=(sent, sent, jax.ShapeDtypeStruct((SLOTS, 4, 128), f32)),
        in_specs=[HBM] * 3,
        out_specs=(HBM,) * 3,
        scratch_shapes=[
            pltpu.VMEM((LEAVES, NRHS, 128), f32),
            pltpu.VMEM((LEAVES, RANK, 128), bf16),
            pltpu.VMEM((85, RANK * RANK), f32),
            pltpu.VMEM((11, 64, 128), f32),
            pltpu.VMEM((TILES, NRHS, 128), f32),
            pltpu.VMEM((SLOTS, 4, 128), f32),
            pltpu.SemaphoreType.DMA((8,)),
        ],
        compiler_params=PARAMS,
        name="moments",
    )(density, basis, transfer)


def local_kernel(
    count,
    near_rows,
    near_cols,
    far_src,
    density_in,
    mine_in,
    before_in,
    after_in,
    tiles_in,
    coupling_in,
    near_out,
    field_out,
    near,
    field,
    density,
    mine,
    before,
    after,
    tiles,
    coupling,
    cells,
    terms,
    rows,
    found,
    places,
    sources,
    semaphores,
    tile_semaphores,
):
    live = count[0]
    step = 16
    turns = (live + step - 1) // step
    device = own_index()
    copies = start_copies(
        [(density_in, density), (before_in, before), (after_in, after), (mine_in, mine)],
        semaphores,
    )

    def tile_copy(turn):
        part = pl.ds(turn * step, step)
        return pltpu.make_async_copy(tiles_in.at[part], tiles.at[part], tile_semaphores.at[turn])

    for turn in range(SLOTS // step):

        @pl.when(turn < turns)
        def _():
            tile_copy(turn).start()

    link_copy = pltpu.make_async_copy(coupling_in, coupling, semaphores.at[4])
    link_copy.start()

    cluster = lax.broadcasted_iota(jnp.int32, (FAR, 85), 1)

    def per_level(values):
        return jnp.where(
            cluster < 64,
            values[0],
            jnp.where(cluster < 80, values[1], jnp.where(cluster < 84, values[2], values[3])),
        )

    named = far_src[...]
    owner = lax.shift_right_logical(named, per_level((6, 4, 2, 0))) - (device - 1)
    within = named & per_level((63, 15, 3, 0))
    places[...] = owner * SPAN + per_level(STARTS) + within
    place_copy = pltpu.make_async_copy(places, sources, semaphores.at[5])
    place_copy.start()

    group8 = lane_groups(8)
    near[...] = jnp.zeros_like(near)
    for copy in copies:
        copy.wait()

    def fill_cells(i, carry):
        for u in range(4):
            cells[i * 4 + u] = stacked(before[i * 4 + u])
            cells[HALO + LEAVES + i * 4 + u] = stacked(after[i * 4 + u])
        for u in range(8):
            cells[HALO + i * 8 + u] = stacked(density[i * 8 + u])
        return carry

    lax.fori_loop(0, 8, fill_cells, 0)

    spread = spreading()
    for place, origin in enumerate((before, mine, after)):

        for first in (0, TILES // 2):
            half = TILES // 2
            both = stacked(origin[HALO + first : HALO + first + half].reshape(16 * half, 128))
            wide = dot_nn(both, spread).astype(bf16)
            for t in range(half):
                for b in range(4):
                    lanes = slice(b * 128, (b + 1) * 128)
                    at = place * SPAN + (first + t) * 4 + b
                    low = 16 * (half + t)
                    terms[at, 0:16] = wide[16 * t : 16 * t + 16, lanes]
                    terms[at, 16:32] = wide[low : low + 16, lanes]

    first_row = device * LEAVES
    first_col = first_row - HALO

    def near_step(turn, carry):
        tile_copy(turn).wait()
        products = []
        for u in range(step):
            slot = turn * step + u
            product = folded(dot_nt(cells[near_cols[slot] - first_col], tiles[slot]))
            products.append(jnp.where(slot < live, product, 0.0))
        for u in range(step):
            row = near_rows[turn * step + u] - first_row
            near[row] = near[row] + products[u]
        return carry

    lax.fori_loop(0, turns, near_step, 0)
    near_copy = pltpu.make_async_copy(near, near_out, semaphores.at[6])
    near_copy.start()
    place_copy.wait()
    link_copy.wait()

    def couple(first, size):
        base = first if isinstance(first, int) else pl.multiple_of(first, 16)
        for j in range(FAR):
            block = coupling[j, pl.ds(base, size), :].astype(f32)
            for half in range(0, size, 8):
                count8 = min(8, size - half)
                for g in range(8):
                    rows[j, half // 8, g * 8 : g * 8 + count8, :] = block[
                        half : half + count8, g * 128 : (g + 1) * 128
                    ]
        for c in range(size):
            total = jnp.zeros((32, 32), f32)
            for j in range(0, FAR, 2):
                pair = range(j, min(j + 2, FAR))
                left = [
                    masked_rows(
                        rows[jj, c // 8, pl.ds(c % 8, 8, stride=8), :], group8
                    ).astype(bf16)
                    for jj in pair
                ]
                right = [terms[sources[jj, first + c]] for jj in pair]
                total = total + dot_nt(
                    jnp.concatenate(right, axis=1), jnp.concatenate(left, axis=1)
                )
            found[first + c] = folded(total)

    def couple_step(i, carry):
        couple(i * 16, 16)
        return carry

    lax.fori_loop(0, 5, couple_step, 0)
    couple(80, 5)
    for i in range(TILES - 1):
        field[i] = jnp.concatenate([found[4 * i + b] for b in range(4)], axis=1)
    field[TILES - 1] = jnp.concatenate([found[84], jnp.zeros((NRHS, 96), f32)], axis=1)
    field_copy = pltpu.make_async_copy(field, field_out, semaphores.at[7])
    field_copy.start()
    near_copy.wait()
    field_copy.wait()


def local_call(count, near_rows, near_cols, far_src, density, mine, before, after, tiles, coupling):
    sent = pltpu.VMEM((HALO + TILES, NRHS, 128), f32)
    return pl.pallas_call(
        local_kernel,
        out_shape=(
            jax.ShapeDtypeStruct((LEAVES, NRHS, 128), f32),
            jax.ShapeDtypeStruct((TILES, NRHS, 128), f32),
        ),
        in_specs=[SMEM] * 3 + [VMEM] + [HBM] * 6,
        out_specs=(HBM, HBM),
        scratch_shapes=[
            pltpu.VMEM((LEAVES, NRHS, 128), f32),
            pltpu.VMEM((TILES, NRHS, 128), f32),
            pltpu.VMEM((LEAVES, NRHS, 128), f32),
            sent,
            sent,
            sent,
            pltpu.VMEM((SLOTS, 128, 128), bf16),
            pltpu.VMEM((FAR, 85, RANK * RANK), bf16),
            pltpu.VMEM((2 * HALO + LEAVES, 2 * NRHS, 128), bf16),
            pltpu.VMEM((3 * SPAN, 2 * NRHS, 128), bf16),
            pltpu.VMEM((FAR, 2, 64, 128), f32),
            pltpu.VMEM((85, NRHS, RANK), f32),
            pltpu.VMEM((FAR, 85), jnp.int32),
            pltpu.SMEM((FAR, 85), jnp.int32),
            pltpu.SemaphoreType.DMA((8,)),
            pltpu.SemaphoreType.DMA((8,)),
        ],
        cost_estimate=pl.CostEstimate(
            flops=LOCAL_FLOPS, bytes_accessed=40_000_000, transcendentals=0
        ),
        compiler_params=PARAMS,
        name="local",
    )(count, near_rows, near_cols, far_src, density, mine, before, after, tiles, coupling)


def crown_kernel(
    sources,
    terms_in,
    field_in,
    near_in,
    coupling_in,
    transfer_top_in,
    transfer_in,
    basis_in,
    out_hbm,
    out,
    given,
    field,
    near,
    coupling,
    transfer_top,
    transfer,
    basis,
    top_rows,
    own_rows,
    link_rows,
    terms,
    semaphores,
):
    copies = start_copies(
        [
            (transfer_top_in, transfer_top),
            (coupling_in, coupling),
            (transfer_in, transfer),
            (basis_in, basis),
            (terms_in, given),
            (field_in, field),
            (near_in, near),
        ],
        semaphores,
    )
    device = own_index()
    place = (device // 4, device // 16, device // 64)
    group8, group16 = lane_groups(8), lane_groups(16)
    mix, spread, gather, unmix = mixing(), spreading(), gathering(), unmixing()
    copies[0].wait()
    spread_rows(transfer_top, 42, top_rows)
    copies[4].wait()
    cells = []
    for c in range(32):
        cells.append((given[4 * c] + given[4 * c + 1]) + (given[4 * c + 2] + given[4 * c + 3]))
    tiled = []
    for c in range(0, 32, 2):
        pair = jnp.concatenate([cells[c], cells[c + 1]], axis=0)
        turned = [pair] + [pltpu.roll(pair, 32 * i, 1) for i in range(1, 4)]
        filled = [by_group([turned[(i - b) % 4] for i in range(4)], group8) for b in range(4)]
        for half in range(2):
            rows4 = slice(4 * half, 4 * half + 4)
            tiled.append(jnp.concatenate([part[rows4] for part in filled], axis=0))
            terms[c + half] = stacked(tiled[c + half])
    packed = [
        stacked(by_group([tiled[4 * i + b] for b in range(4)], group16)) for i in range(8)
    ]
    mixed = dot_nn(jnp.concatenate(packed, axis=0), mix).astype(bf16)
    pairs = [(mixed[32 * i : 32 * i + 16], mixed[32 * i + 16 : 32 * i + 32]) for i in range(8)]
    for size, start, at in ((32, 0, 32), (8, 32, 40)):
        raised = [
            lifted(pairs[i][0], pairs[i][1], family(top_rows, start + 4 * i, 4, group8))
            for i in range(size // 4)
        ]
        pairs = []
        for i in range(0, size // 4, 4):
            plain, mixed = gathered(raised[i : i + 4], gather)
            pairs.append(halves(mixed))
            wide = dot_nn(stacked(plain), spread).astype(bf16)
            for b in range(min(4, size // 4)):
                terms[at + i + b] = wide[:, b * 128 : (b + 1) * 128]
    copies[1].wait()
    half = pl.multiple_of((place[0] // 16) * 16, 16)
    upper8 = (place[0] % 16) < 8
    for j in range(FAR):
        block = coupling[j, pl.ds(half, 16), :].astype(f32)
        block = jnp.where(upper8, block[0:8], block[8:16])
        last = coupling[j, 32:42, :].astype(f32)
        for g in range(8):
            lanes = slice(g * 128, (g + 1) * 128)
            link_rows[0, j, g * 8 : g * 8 + 8, :] = block[:, lanes]
            link_rows[1, j, g * 8 : g * 8 + 8, :] = last[0:8, lanes]
            link_rows[2, j, g * 8 : g * 8 + 2, :] = last[8:10, lanes]
    fields = []
    for level in range(3):
        total = jnp.zeros((32, 32), f32)
        for j in range(0, FAR, 2):
            pair = range(j, min(j + 2, FAR))
            left = [
                masked_rows(
                    link_rows[level, jj, pl.ds(place[level] % 8, 8, stride=8), :], group8
                ).astype(bf16)
                for jj in pair
            ]
            right = [
                terms[UPPER_STARTS[level] + sources[jj, UPPER_STARTS[level] + place[level]]]
                for jj in pair
            ]
            total = total + dot_nt(jnp.concatenate(right, axis=1), jnp.concatenate(left, axis=1))
        fields.append(folded(total))

    def one_tiled(mixed):
        padded = jnp.concatenate([mixed, jnp.zeros((NRHS, 96), f32)], axis=1)
        return folded(dot_nn(stacked(padded), unmix[:, 0:128]))

    def top_family(index):
        rows8 = top_rows[index // 8, pl.ds(index % 8, 8, stride=8), :]
        return halves(masked_rows(rows8, group8))

    coeffs = one_tiled(fields[2])
    coeffs = one_tiled(fields[1] + lowered(coeffs, top_family(UPPER_STARTS[1] + place[1])))
    coeffs = one_tiled(fields[0] + lowered(coeffs, top_family(UPPER_STARTS[0] + place[0])))
    copies[2].wait()
    spread_rows(transfer, 85, own_rows)
    copies[5].wait()
    parents = [coeffs]
    tile = TILES - 1
    for size, start in ((1, 84), (4, 80), (16, 64), (64, 0)):
        tiles_here = (size + 3) // 4
        first = tile - tiles_here + 1
        mixed = []
        for i in range(tiles_here):
            matrices = family(own_rows, start + 4 * i, min(4, size), group8)
            mixed.append(field[first + i] + lowered(parents[i], matrices))
        if size == 64:
            break
        wide = folded(dot_nn(stacked(jnp.concatenate(mixed, axis=0)), unmix))
        children = [
            wide[16 * i : 16 * i + 16, b * 128 : (b + 1) * 128]
            for i in range(tiles_here)
            for b in range(min(4, size))
        ]
        parents = children
        tile = first - 1
    plain = folded(dot_nn(stacked(jnp.concatenate(mixed, axis=0)), unmixing_one()))
    copies[3].wait()
    copies[6].wait()
    sent = []
    for i in range(16):
        packed = plain[16 * i : 16 * i + 16]
        blocks = [jnp.where(group16 == b, packed, 0.0) for b in range(4)]
        far = folded(
            dot_nn(
                stacked(jnp.concatenate(blocks, axis=0)),
                basis[4 * i : 4 * i + 4].reshape(128, 128),
            )
        )
        out[4 * i : 4 * i + 4] = near[4 * i : 4 * i + 4] + far.reshape(4, NRHS, 128)
        if i % 4 == 3:
            part = pl.ds(4 * i - 12, 16)
            sent.append(
                pltpu.make_async_copy(out.at[part], out_hbm.at[part], semaphores.at[7 + i // 4])
            )
            sent[-1].start()
    for copy in sent:
        copy.wait()


def crown_call(sources, terms, field, near, coupling_top, transfer_top, transfer, basis):
    return pl.pallas_call(
        crown_kernel,
        out_shape=jax.ShapeDtypeStruct((LEAVES, NRHS, 128), f32),
        in_specs=[SMEM] + [HBM] * 7,
        out_specs=HBM,
        scratch_shapes=[
            pltpu.VMEM((LEAVES, NRHS, 128), f32),
            pltpu.VMEM((SLOTS, 4, 128), f32),
            pltpu.VMEM((TILES, NRHS, 128), f32),
            pltpu.VMEM((LEAVES, NRHS, 128), f32),
            pltpu.VMEM((FAR, 42, RANK * RANK), bf16),
            pltpu.VMEM((42, RANK * RANK), f32),
            pltpu.VMEM((85, RANK * RANK), f32),
            pltpu.VMEM((LEAVES, RANK, 128), bf16),
            pltpu.VMEM((6, 64, 128), f32),
            pltpu.VMEM((11, 64, 128), f32),
            pltpu.VMEM((3, FAR, 64, 128), f32),
            pltpu.VMEM((42, 32, 128), bf16),
            pltpu.SemaphoreType.DMA((11,)),
        ],
        compiler_params=PARAMS,
        name="crown",
    )(sources, terms, field, near, coupling_top, transfer_top, transfer, basis)


def body(
    density,
    leaf_basis,
    near_tiles,
    near_rows,
    near_cols,
    near_count,
    far_src,
    coupling,
    transfer,
    far_src_top,
    coupling_top,
    transfer_top,
):
    devices = lax.axis_size("leaf") * lax.axis_size("sub")
    right, left, crown = moments_call(density, leaf_basis, transfer)
    before = lax.ppermute(right, AXES, [(i, (i + 1) % devices) for i in range(devices)])
    after = lax.ppermute(left, AXES, [((i + 1) % devices, i) for i in range(devices)])
    terms = lax.all_to_all(crown, AXES, 0, 0, tiled=True)
    near, field = local_call(
        near_count,
        near_rows,
        near_cols,
        far_src.T,
        density,
        right,
        before,
        after,
        near_tiles,
        coupling,
    )
    return crown_call(
        far_src_top.T,
        terms,
        field,
        near,
        jnp.transpose(coupling_top, (1, 0, 2)),
        transfer_top,
        transfer,
        leaf_basis,
    )


def solution(mesh):
    placed = (
        P(AXES, None, None),
        P(AXES, None, None),
        P(AXES, None, None),
        P(AXES),
        P(AXES),
        P(AXES),
        P(AXES, None),
        P(None, AXES, None),
        P(AXES, None),
        P(),
        P(),
        P(),
    )
    return jax.shard_map(
        body, mesh=mesh, in_specs=placed, out_specs=P(AXES, None, None), check_vma=False
    )
```

```python
import jax
import jax.numpy as jnp
from jax import lax
from jax.experimental import pallas as pl
from jax.experimental.pallas import tpu as pltpu
from jax.sharding import PartitionSpec as P

f32, bf16 = jnp.float32, jnp.bfloat16
AXES = ("leaf", "sub")
LEAVES = 64
HALO = 32
NRHS = 16
RANK = 32
FAR = 27
SLOTS = 128
LEVELS = (64, 16, 4, 1)
STARTS = (0, 64, 80, 84)
UPPER = (32, 8, 2)
UPPER_STARTS = (0, 32, 40)
TILES = 22
SPAN = 4 * TILES
LOCAL_FLOPS = 2_000_000_000
PARAMS = pltpu.CompilerParams(vmem_limit_bytes=60 * 1024 * 1024)


def dot_nn(a, b):
    return lax.dot_general(a, b, (((1,), (0,)), ((), ())), preferred_element_type=f32)


def dot_nt(a, b):
    return lax.dot_general(a, b, (((1,), (1,)), ((), ())), preferred_element_type=f32)


def halves(x):
    high = x.astype(bf16)
    return high, (x - high.astype(f32)).astype(bf16)


def stacked(x):
    high, low = halves(x)
    return jnp.concatenate([high, low], axis=0)


def folded(x):
    half = x.shape[0] // 2
    return x[:half] + x[half:]


def grid_of(shape):
    return (
        lax.broadcasted_iota(jnp.int32, shape, 0),
        lax.broadcasted_iota(jnp.int32, shape, 1),
    )


def ones_where(mask):
    return jnp.where(mask, 1.0, 0.0).astype(bf16)


def natural_of(lane):
    return (lane // 32) * 32 + 4 * (lane % 8) + (lane % 32) // 8


def mixing():
    x, y = grid_of((128, 128))
    return ones_where(x == natural_of(y))


def spreading():
    x, y = grid_of((128, 512))
    return ones_where((x // 32 == y // 128) & (x % 32 == y % 32))


def unmixing():
    x, y = grid_of((128, 512))
    return ones_where((x // 32 == y // 128) & (natural_of(x) % 32 == y % 32))


def unmixing_one():
    x, y = grid_of((128, 128))
    return ones_where(y == natural_of(x))


def gathering():
    x, y = grid_of((512, 256))
    lane = y % 128
    entry = jnp.where(y < 128, lane % 32, natural_of(lane) % 32)
    return ones_where((lane // 32 == x // 128) & (entry == x % 32))


def tiling():
    x, y = grid_of((128, 128))
    return ones_where(x % 32 == y % 32)


def lane_groups(rows):
    return lax.broadcasted_iota(jnp.int32, (rows, 128), 1) // 32


def by_group(parts, group):
    out = parts[0]
    for index in range(1, len(parts)):
        out = jnp.where(group == index, parts[index], out)
    return out


def spread_rows(matrix_ref, rows, scratch):
    for first in range(0, rows, 8):
        count = min(8, rows - first)
        block = matrix_ref[first : first + count, :].astype(f32)
        for g in range(8):
            scratch[first // 8, g * 8 : g * 8 + count, :] = block[:, g * 128 : (g + 1) * 128]


def row_of(scratch, row):
    return scratch[row // 8, pl.ds(row % 8, 8, stride=8), :]


def masked_rows(rows8, group8):
    return jnp.concatenate([jnp.where(group8 == r, rows8, 0.0) for r in range(4)], axis=0)


def family(scratch, first, count, group8):
    blocks = [masked_rows(row_of(scratch, first + b), group8) for b in range(count)]
    if count < 4:
        blocks.append(jnp.zeros((32 * (4 - count), 128), f32))
    return halves(jnp.concatenate(blocks, axis=0))


def lifted(high, low, matrices):
    matrix_high, matrix_low = matrices
    return folded(dot_nn(jnp.concatenate([high, low], axis=0), matrix_high)) + dot_nn(
        high, matrix_low
    )


def lowered(coeffs, matrices):
    high, low = halves(coeffs)
    matrix_high, matrix_low = matrices
    return folded(dot_nt(jnp.concatenate([high, low], axis=0), matrix_high)) + dot_nt(
        high, matrix_low
    )


def gathered(parts, gather):
    wide = jnp.concatenate(
        parts + [jnp.zeros((NRHS, 128), f32)] * (4 - len(parts)), axis=1
    )
    both = folded(dot_nn(stacked(wide), gather))
    return both[:, :128], both[:, 128:]


def own_index():
    return lax.axis_index("leaf") * lax.axis_size("sub") + lax.axis_index("sub")


def start_copies(pairs, semaphores):
    copies = [
        pltpu.make_async_copy(source, target, semaphores.at[i])
        for i, (source, target) in enumerate(pairs)
    ]
    for copy in copies:
        copy.start()
    return copies


def moments_kernel(
    density_in,
    basis_in,
    transfer_in,
    right_out,
    left_out,
    crown_out,
    density,
    basis,
    transfer,
    rows,
    summed,
    crown_terms,
    semaphores,
):
    copies = start_copies(
        [
            (density_in, density),
            (basis_in, basis),
            (transfer_in, transfer),
        ],
        semaphores,
    )
    group16, group8 = lane_groups(16), lane_groups(8)
    mix = mixing()
    gather = gathering()
    copies[0].wait()
    for i, (target, first) in enumerate(((right_out, LEAVES - HALO), (left_out, 0))):
        copy = pltpu.make_async_copy(
            density.at[pl.ds(first, HALO)], target.at[pl.ds(0, HALO)], semaphores.at[3 + i]
        )
        copy.start()
        copies.append(copy)
    copies[1].wait()
    natural = []
    for i in range(16):
        cells = density[4 * i : 4 * i + 4].reshape(64, 128)
        wide = basis[4 * i : 4 * i + 4].reshape(128, 128)
        found = folded(dot_nt(stacked(cells), wide))
        natural.append(by_group([found[16 * b : 16 * b + 16] for b in range(4)], group16))
    level = jnp.concatenate(natural, axis=0)
    high, low = halves(level)
    high, low = dot_nn(high, mix).astype(bf16), dot_nn(low, mix).astype(bf16)
    tile = 0
    for part in natural:
        summed[tile] = part
        tile += 1
    copies[2].wait()
    spread_rows(transfer, 85, rows)
    pairs = [(high[16 * i : 16 * i + 16], low[16 * i : 16 * i + 16]) for i in range(16)]
    for size, start in ((64, 0), (16, 64), (4, 80)):
        raised = [
            lifted(pairs[i][0], pairs[i][1], family(rows, start + 4 * i, 4, group8))
            for i in range(size // 4)
        ]
        pairs = []
        for i in range(0, size // 4, 4):
            plain, mixed = gathered(raised[i : i + 4], gather)
            summed[tile] = plain
            tile += 1
            pairs.append(halves(mixed))
    for i, target in enumerate((right_out, left_out)):
        copy = pltpu.make_async_copy(
            summed, target.at[pl.ds(HALO, TILES)], semaphores.at[5 + i]
        )
        copy.start()
        copies.append(copy)
    crown = lifted(pairs[0][0], pairs[0][1], family(rows, 84, 1, group8))
    crown = folded(dot_nn(stacked(crown), tiling()))
    packed = by_group([crown[4 * b : 4 * b + 4] for b in range(4)], lane_groups(4))
    for i in range(SLOTS):
        crown_terms[i] = packed
    last = pltpu.make_async_copy(crown_terms, crown_out, semaphores.at[7])
    last.start()
    for copy in copies[3:] + [last]:
        copy.wait()


HBM = pl.BlockSpec(memory_space=pltpu.HBM)
VMEM = pl.BlockSpec(memory_space=pltpu.VMEM)
SMEM = pl.BlockSpec(memory_space=pltpu.SMEM)


def moments_call(density, basis, transfer):
    sent = jax.ShapeDtypeStruct((HALO + TILES, NRHS, 128), f32)
    return pl.pallas_call(
        moments_kernel,
        out_shape=(sent, sent, jax.ShapeDtypeStruct((SLOTS, 4, 128), f32)),
        in_specs=[HBM] * 3,
        out_specs=(HBM,) * 3,
        scratch_shapes=[
            pltpu.VMEM((LEAVES, NRHS, 128), f32),
            pltpu.VMEM((LEAVES, RANK, 128), bf16),
            pltpu.VMEM((85, RANK * RANK), f32),
            pltpu.VMEM((11, 64, 128), f32),
            pltpu.VMEM((TILES, NRHS, 128), f32),
            pltpu.VMEM((SLOTS, 4, 128), f32),
            pltpu.SemaphoreType.DMA((8,)),
        ],
        compiler_params=PARAMS,
        name="moments",
    )(density, basis, transfer)


def local_kernel(
    count,
    near_rows,
    near_cols,
    far_src,
    density_in,
    mine_in,
    before_in,
    after_in,
    tiles_in,
    coupling_in,
    near_out,
    field_out,
    near,
    field,
    density,
    mine,
    before,
    after,
    tiles,
    coupling,
    cells,
    terms,
    rows,
    found,
    places,
    sources,
    semaphores,
    tile_semaphores,
):
    live = count[0]
    step = 32
    turns = (live + step - 1) // step
    device = own_index()
    copies = start_copies(
        [(density_in, density), (before_in, before), (after_in, after), (mine_in, mine)],
        semaphores,
    )

    def tile_copy(turn):
        part = pl.ds(turn * step, step)
        return pltpu.make_async_copy(tiles_in.at[part], tiles.at[part], tile_semaphores.at[turn])

    for turn in range(SLOTS // step):

        @pl.when(turn < turns)
        def _():
            tile_copy(turn).start()

    link_copy = pltpu.make_async_copy(coupling_in, coupling, semaphores.at[4])
    link_copy.start()

    cluster = lax.broadcasted_iota(jnp.int32, (FAR, 85), 1)

    def per_level(values):
        return jnp.where(
            cluster < 64,
            values[0],
            jnp.where(cluster < 80, values[1], jnp.where(cluster < 84, values[2], values[3])),
        )

    named = far_src[...]
    owner = lax.shift_right_logical(named, per_level((6, 4, 2, 0))) - (device - 1)
    within = named & per_level((63, 15, 3, 0))
    places[...] = owner * SPAN + per_level(STARTS) + within
    place_copy = pltpu.make_async_copy(places, sources, semaphores.at[5])
    place_copy.start()

    group8 = lane_groups(8)
    near[...] = jnp.zeros_like(near)
    for copy in copies:
        copy.wait()

    def fill_cells(i, carry):
        for u in range(4):
            cells[i * 4 + u] = stacked(before[i * 4 + u])
            cells[HALO + LEAVES + i * 4 + u] = stacked(after[i * 4 + u])
        for u in range(8):
            cells[HALO + i * 8 + u] = stacked(density[i * 8 + u])
        return carry

    lax.fori_loop(0, 8, fill_cells, 0)

    spread = spreading()
    for place, origin in enumerate((before, mine, after)):

        for first in (0, TILES // 2):
            half = TILES // 2
            both = stacked(origin[HALO + first : HALO + first + half].reshape(16 * half, 128))
            wide = dot_nn(both, spread).astype(bf16)
            for t in range(half):
                for b in range(4):
                    lanes = slice(b * 128, (b + 1) * 128)
                    at = place * SPAN + (first + t) * 4 + b
                    low = 16 * (half + t)
                    terms[at, 0:16] = wide[16 * t : 16 * t + 16, lanes]
                    terms[at, 16:32] = wide[low : low + 16, lanes]

    first_row = device * LEAVES
    first_col = first_row - HALO

    def near_step(turn, carry):
        tile_copy(turn).wait()
        products = []
        for u in range(step):
            slot = turn * step + u
            product = folded(dot_nt(cells[near_cols[slot] - first_col], tiles[slot]))
            products.append(jnp.where(slot < live, product, 0.0))
        for u in range(step):
            row = near_rows[turn * step + u] - first_row
            near[row] = near[row] + products[u]
        return carry

    lax.fori_loop(0, turns, near_step, 0)
    near_copy = pltpu.make_async_copy(near, near_out, semaphores.at[6])
    near_copy.start()
    place_copy.wait()
    link_copy.wait()

    def couple(first, size):
        base = first if isinstance(first, int) else pl.multiple_of(first, 16)
        for j in range(FAR):
            block = coupling[j, pl.ds(base, size), :].astype(f32)
            for half in range(0, size, 8):
                count8 = min(8, size - half)
                for g in range(8):
                    rows[j, half // 8, g * 8 : g * 8 + count8, :] = block[
                        half : half + count8, g * 128 : (g + 1) * 128
                    ]
        for c in range(size):
            total = jnp.zeros((32, 32), f32)
            for j in range(0, FAR, 2):
                pair = range(j, min(j + 2, FAR))
                left = [
                    masked_rows(
                        rows[jj, c // 8, pl.ds(c % 8, 8, stride=8), :], group8
                    ).astype(bf16)
                    for jj in pair
                ]
                right = [terms[sources[jj, first + c]] for jj in pair]
                total = total + dot_nt(
                    jnp.concatenate(right, axis=1), jnp.concatenate(left, axis=1)
                )
            found[first + c] = folded(total)

    def couple_step(i, carry):
        couple(i * 32, 32)
        return carry

    lax.fori_loop(0, 2, couple_step, 0)
    couple(64, 21)
    for i in range(TILES - 1):
        field[i] = jnp.concatenate([found[4 * i + b] for b in range(4)], axis=1)
    field[TILES - 1] = jnp.concatenate([found[84], jnp.zeros((NRHS, 96), f32)], axis=1)
    field_copy = pltpu.make_async_copy(field, field_out, semaphores.at[7])
    field_copy.start()
    near_copy.wait()
    field_copy.wait()


def local_call(count, near_rows, near_cols, far_src, density, mine, before, after, tiles, coupling):
    sent = pltpu.VMEM((HALO + TILES, NRHS, 128), f32)
    return pl.pallas_call(
        local_kernel,
        out_shape=(
            jax.ShapeDtypeStruct((LEAVES, NRHS, 128), f32),
            jax.ShapeDtypeStruct((TILES, NRHS, 128), f32),
        ),
        in_specs=[SMEM] * 3 + [VMEM] + [HBM] * 6,
        out_specs=(HBM, HBM),
        scratch_shapes=[
            pltpu.VMEM((LEAVES, NRHS, 128), f32),
            pltpu.VMEM((TILES, NRHS, 128), f32),
            pltpu.VMEM((LEAVES, NRHS, 128), f32),
            sent,
            sent,
            sent,
            pltpu.VMEM((SLOTS, 128, 128), bf16),
            pltpu.VMEM((FAR, 85, RANK * RANK), bf16),
            pltpu.VMEM((2 * HALO + LEAVES, 2 * NRHS, 128), bf16),
            pltpu.VMEM((3 * SPAN, 2 * NRHS, 128), bf16),
            pltpu.VMEM((FAR, 4, 64, 128), f32),
            pltpu.VMEM((85, NRHS, RANK), f32),
            pltpu.VMEM((FAR, 85), jnp.int32),
            pltpu.SMEM((FAR, 85), jnp.int32),
            pltpu.SemaphoreType.DMA((8,)),
            pltpu.SemaphoreType.DMA((8,)),
        ],
        cost_estimate=pl.CostEstimate(
            flops=LOCAL_FLOPS, bytes_accessed=40_000_000, transcendentals=0
        ),
        compiler_params=PARAMS,
        name="local",
    )(count, near_rows, near_cols, far_src, density, mine, before, after, tiles, coupling)


def crown_kernel(
    sources,
    terms_in,
    field_in,
    near_in,
    coupling_in,
    transfer_top_in,
    transfer_in,
    basis_in,
    out_hbm,
    out,
    given,
    field,
    near,
    coupling,
    transfer_top,
    transfer,
    basis,
    top_rows,
    own_rows,
    link_rows,
    terms,
    semaphores,
):
    copies = start_copies(
        [
            (terms_in, given),
            (transfer_top_in, transfer_top),
            (coupling_in, coupling),
            (transfer_in, transfer),
            (field_in, field),
            (basis_in, basis),
            (near_in, near),
        ],
        semaphores,
    )
    device = own_index()
    place = (device // 4, device // 16, device // 64)
    group8, group16 = lane_groups(8), lane_groups(16)
    mix, spread, gather, unmix = mixing(), spreading(), gathering(), unmixing()
    copies[1].wait()
    spread_rows(transfer_top, 42, top_rows)
    copies[0].wait()
    cells = []
    for c in range(32):
        cells.append((given[4 * c] + given[4 * c + 1]) + (given[4 * c + 2] + given[4 * c + 3]))
    tiled = []
    for c in range(0, 32, 2):
        pair = jnp.concatenate([cells[c], cells[c + 1]], axis=0)
        turned = [pair] + [pltpu.roll(pair, 32 * i, 1) for i in range(1, 4)]
        filled = [by_group([turned[(i - b) % 4] for i in range(4)], group8) for b in range(4)]
        for half in range(2):
            rows4 = slice(4 * half, 4 * half + 4)
            tiled.append(jnp.concatenate([part[rows4] for part in filled], axis=0))
            terms[c + half] = stacked(tiled[c + half])
    packed = [
        stacked(by_group([tiled[4 * i + b] for b in range(4)], group16)) for i in range(8)
    ]
    mixed = dot_nn(jnp.concatenate(packed, axis=0), mix).astype(bf16)
    pairs = [(mixed[32 * i : 32 * i + 16], mixed[32 * i + 16 : 32 * i + 32]) for i in range(8)]
    for size, start, at in ((32, 0, 32), (8, 32, 40)):
        raised = [
            lifted(pairs[i][0], pairs[i][1], family(top_rows, start + 4 * i, 4, group8))
            for i in range(size // 4)
        ]
        pairs = []
        for i in range(0, size // 4, 4):
            plain, mixed = gathered(raised[i : i + 4], gather)
            pairs.append(halves(mixed))
            wide = dot_nn(stacked(plain), spread).astype(bf16)
            for b in range(min(4, size // 4)):
                terms[at + i + b] = wide[:, b * 128 : (b + 1) * 128]
    copies[2].wait()
    half = pl.multiple_of((place[0] // 16) * 16, 16)
    upper8 = (place[0] % 16) < 8
    for j in range(FAR):
        block = coupling[j, pl.ds(half, 16), :].astype(f32)
        block = jnp.where(upper8, block[0:8], block[8:16])
        last = coupling[j, 32:42, :].astype(f32)
        for g in range(8):
            lanes = slice(g * 128, (g + 1) * 128)
            link_rows[0, j, g * 8 : g * 8 + 8, :] = block[:, lanes]
            link_rows[1, j, g * 8 : g * 8 + 8, :] = last[0:8, lanes]
            link_rows[2, j, g * 8 : g * 8 + 2, :] = last[8:10, lanes]
    fields = []
    for level in range(3):
        total = jnp.zeros((32, 32), f32)
        for j in range(0, FAR, 2):
            pair = range(j, min(j + 2, FAR))
            left = [
                masked_rows(
                    link_rows[level, jj, pl.ds(place[level] % 8, 8, stride=8), :], group8
                ).astype(bf16)
                for jj in pair
            ]
            right = [
                terms[UPPER_STARTS[level] + sources[jj, UPPER_STARTS[level] + place[level]]]
                for jj in pair
            ]
            total = total + dot_nt(jnp.concatenate(right, axis=1), jnp.concatenate(left, axis=1))
        fields.append(folded(total))

    def one_tiled(mixed):
        padded = jnp.concatenate([mixed, jnp.zeros((NRHS, 96), f32)], axis=1)
        return folded(dot_nn(stacked(padded), unmix[:, 0:128]))

    def top_family(index):
        rows8 = top_rows[index // 8, pl.ds(index % 8, 8, stride=8), :]
        return halves(masked_rows(rows8, group8))

    coeffs = one_tiled(fields[2])
    coeffs = one_tiled(fields[1] + lowered(coeffs, top_family(UPPER_STARTS[1] + place[1])))
    coeffs = one_tiled(fields[0] + lowered(coeffs, top_family(UPPER_STARTS[0] + place[0])))
    copies[3].wait()
    spread_rows(transfer, 85, own_rows)
    copies[4].wait()
    parents = [coeffs]
    tile = TILES - 1
    for size, start in ((1, 84), (4, 80), (16, 64), (64, 0)):
        tiles_here = (size + 3) // 4
        first = tile - tiles_here + 1
        mixed = []
        for i in range(tiles_here):
            matrices = family(own_rows, start + 4 * i, min(4, size), group8)
            mixed.append(field[first + i] + lowered(parents[i], matrices))
        if size == 64:
            break
        wide = folded(dot_nn(stacked(jnp.concatenate(mixed, axis=0)), unmix))
        children = [
            wide[16 * i : 16 * i + 16, b * 128 : (b + 1) * 128]
            for i in range(tiles_here)
            for b in range(min(4, size))
        ]
        parents = children
        tile = first - 1
    plain = folded(dot_nn(stacked(jnp.concatenate(mixed, axis=0)), unmixing_one()))
    copies[5].wait()
    copies[6].wait()
    sent = []
    for i in range(16):
        packed = plain[16 * i : 16 * i + 16]
        blocks = [jnp.where(group16 == b, packed, 0.0) for b in range(4)]
        far = folded(
            dot_nn(
                stacked(jnp.concatenate(blocks, axis=0)),
                basis[4 * i : 4 * i + 4].reshape(128, 128),
            )
        )
        out[4 * i : 4 * i + 4] = near[4 * i : 4 * i + 4] + far.reshape(4, NRHS, 128)
        if i % 4 == 3:
            part = pl.ds(4 * i - 12, 16)
            sent.append(
                pltpu.make_async_copy(out.at[part], out_hbm.at[part], semaphores.at[7 + i // 4])
            )
            sent[-1].start()
    for copy in sent:
        copy.wait()


def crown_call(sources, terms, field, near, coupling_top, transfer_top, transfer, basis):
    return pl.pallas_call(
        crown_kernel,
        out_shape=jax.ShapeDtypeStruct((LEAVES, NRHS, 128), f32),
        in_specs=[SMEM] + [HBM] * 7,
        out_specs=HBM,
        scratch_shapes=[
            pltpu.VMEM((LEAVES, NRHS, 128), f32),
            pltpu.VMEM((SLOTS, 4, 128), f32),
            pltpu.VMEM((TILES, NRHS, 128), f32),
            pltpu.VMEM((LEAVES, NRHS, 128), f32),
            pltpu.VMEM((FAR, 42, RANK * RANK), bf16),
            pltpu.VMEM((42, RANK * RANK), f32),
            pltpu.VMEM((85, RANK * RANK), f32),
            pltpu.VMEM((LEAVES, RANK, 128), bf16),
            pltpu.VMEM((6, 64, 128), f32),
            pltpu.VMEM((11, 64, 128), f32),
            pltpu.VMEM((3, FAR, 64, 128), f32),
            pltpu.VMEM((42, 32, 128), bf16),
            pltpu.SemaphoreType.DMA((11,)),
        ],
        compiler_params=PARAMS,
        name="crown",
    )(sources, terms, field, near, coupling_top, transfer_top, transfer, basis)


def body(
    density,
    leaf_basis,
    near_tiles,
    near_rows,
    near_cols,
    near_count,
    far_src,
    coupling,
    transfer,
    far_src_top,
    coupling_top,
    transfer_top,
):
    devices = lax.axis_size("leaf") * lax.axis_size("sub")
    right, left, crown = moments_call(density, leaf_basis, transfer)
    before = lax.ppermute(right, AXES, [(i, (i + 1) % devices) for i in range(devices)])
    after = lax.ppermute(left, AXES, [((i + 1) % devices, i) for i in range(devices)])
    terms = lax.all_to_all(crown, AXES, 0, 0, tiled=True)
    near, field = local_call(
        near_count,
        near_rows,
        near_cols,
        far_src.T,
        density,
        right,
        before,
        after,
        near_tiles,
        coupling,
    )
    return crown_call(
        far_src_top.T,
        terms,
        field,
        near,
        jnp.transpose(coupling_top, (1, 0, 2)),
        transfer_top,
        transfer,
        leaf_basis,
    )


def solution(mesh):
    placed = (
        P(AXES, None, None),
        P(AXES, None, None),
        P(AXES, None, None),
        P(AXES),
        P(AXES),
        P(AXES),
        P(AXES, None),
        P(None, AXES, None),
        P(AXES, None),
        P(),
        P(),
        P(),
    )
    return jax.shard_map(
        body, mesh=mesh, in_specs=placed, out_specs=P(AXES, None, None), check_vma=False
    )
```
